128 devices in a mesh: ctx: 8 (over y, z_lo), tp: 16 (over x, z_hi, core).
Axes of the slice: x: 4, y: 4, z: 4 (z_hi: 2, z_lo: 2; z = z_hi * 2 + z_lo), core: 2. Of those that a mesh axis runs over, the one named last changes fastest.
Arguments:
- context: bfloat16 [16384, 4096], P('ctx', 'tp'), may hold values from -6 to 6
- residual: bfloat16 [16384, 2048], P(('ctx', 'tp')), may hold values from -6 to 6
- o_weight: bfloat16 [4096, 2048], P('tp'), may hold values from -0.09375 to 0.09375
- norm_gain: bfloat16 [2048], replicated, may hold values from 0.099609375 to 1.8984375
- routes: int32 [16384, 4], P(('ctx', 'tp')), may hold values from 0 to 127, all different within a row; in each aligned block of 128 rows (0 to 127, 128 to 255, ...) at most 6 rows name the same one
- gate_weights: float32 [16384, 4], P(('ctx', 'tp')), may hold values from 0.05 to 0.5
- expert_in: bfloat16 [128, 2048, 1536], P(('ctx', 'tp')), may hold values from -0.125 to 0.125
- expert_out: bfloat16 [128, 768, 2048], P(('ctx', 'tp')), may hold values from -0.21875 to 0.21875
- cotangent: bfloat16 [16384, 2048], P(('ctx', 'tp')), may hold values from -6 to 6
Outputs:
- layer_out: bfloat16 [16384, 2048], P(('ctx', 'tp'))
- d_context: bfloat16 [16384, 4096], P('ctx', 'tp')
- d_residual: bfloat16 [16384, 2048], P(('ctx', 'tp'))
- d_o_weight: float32 [4096, 2048], P('tp', 'ctx')
- d_gain: float32 [2048], replicated
- d_expert_in: bfloat16 [128, 2048, 1536], P(('ctx', 'tp'))
- d_expert_out: bfloat16 [128, 768, 2048], P(('ctx', 'tp'))
The draws below stay inside these ranges and needn't reach their ends.
Inputs may be any that keep to these rules, and one draw needn't show every extreme that they name: `routes`: each token names 4 different experts; the 128 tokens of one device (aligned blocks) name one expert at most 6 times, a bound that some block reaches.
All inputs are finite; a program needn't handle non-finite values.
Results may differ from the reference program's by a relative error of at most 0.019.
Values may be sent and summed in bfloat16 or wider, within the bound.
No kernel may reach another device: no remote copies, remote signals or barrier semaphores. Data moves between devices by JAX's collectives and lax.ppermute only.
A program may use at most 128 MiB of HBM per device.

```python
import math
import jax
import jax.numpy as jnp
import numpy as np
from jax import lax

D = 2048
HEADS = 32
HEAD_DIM = 128
FF = 768
TOK_DEV = 128
ROUTES = 4
EXPERTS = 128
CAP = 6
SEQ = 16384


def steps_of(stream_key, dims, cuts, smallest, top_value):
    def one(dim, blocks):
        steps = jax.random.uniform(jax.random.fold_in(jax.random.fold_in(stream_key, 6), dim), (blocks,), jnp.float32, smallest / len(cuts), top_value / len(cuts))
        return jnp.repeat(jnp.exp(steps), dims[dim] // blocks).reshape((-1,) + (1,) * (len(dims) - dim - 1))

    gain = one(*cuts[0])
    for cut in cuts[1:]:
        gain = gain * one(*cut)
    return gain


def deal_out(key, own, number, rows, count, top, bound, slope):
    order = jax.random.permutation(key, count)
    packed, ordinary = shares(count, rows * top, bound, slope, True), shares(count, rows * top, bound, slope, False)
    places = jnp.arange(count)

    def named(lengths, offset_by):
        used = int((lengths > 0).sum())
        fixed = max(1, used // 4)
        moved = fixed + (places - fixed + offset_by * (used - fixed)) % max(1, count - fixed)
        return jnp.zeros((count,), jnp.int32).at[order[jnp.where(places < fixed, places, moved)]].set(jnp.asarray(lengths, jnp.int32))

    lengths = jnp.where(number % 4 == 0, named(packed, number // 4), named(ordinary, number - number // 4 - 1))
    mixed = jax.random.permutation(jax.random.fold_in(own, 3), count)
    giver, receiver = mixed[0:count // 2 * 2:2], mixed[1:count // 2 * 2:2]
    room = jnp.minimum(lengths[giver] - 1, bound - lengths[receiver]) // 2
    room = jnp.where((giver == order[0]) | (receiver == order[0]) | (lengths[receiver] == 0), 0, jnp.maximum(room, 0))
    moved = jax.random.randint(jax.random.fold_in(own, 4), (count // 2,), 0, 1 << 20) % (room + 1)
    lengths = lengths.at[giver].add(-moved).at[receiver].add(moved)
    items = jnp.searchsorted(jnp.cumsum(lengths), jnp.arange(rows * top), side="right").astype(jnp.int32)
    listing = items.reshape(top, rows).T
    listing = listing[jax.random.permutation(jax.random.fold_in(own, 1), rows)]
    offset_by = jax.random.randint(jax.random.fold_in(own, 2), (rows, 1), 0, top)
    return jnp.take_along_axis(listing, (jnp.arange(top)[None, :] + offset_by) % top, axis=1)


def shares(number_of, total, bound, slope, full):
    weights = [(1 << 20) // math.isqrt(grade ** slope) + 1 for grade in range(1, number_of + 1)]
    largest = bound if full else min(bound, max(-(-total // number_of), total * weights[0] // sum(weights)))
    least = 1 if total - largest >= number_of - 1 else 0
    given, surplus = [largest] + [least] * (number_of - 1), total - largest - least * (number_of - 1)
    while surplus > 0:
        candidates = [i for i in range(1, number_of) if given[i] < largest] or [i for i in range(1, number_of) if given[i] < bound]
        whole, budget = sum([weights[i] for i in candidates]), surplus
        for i in candidates:
            extra = min(bound - given[i], max(1, budget * weights[i] // whole), surplus)
            given[i] = given[i] + extra
            surplus = surplus - extra
    return np.array(given)


def gaussian(key, shape, width, bound, cuts=(), kind=jnp.bfloat16):
    loudness = steps_of(key, shape, cuts, -0.22, 0.18) if cuts else 1.0
    result = jax.random.normal(key, shape, jnp.float32) * width * loudness
    return jnp.minimum(jnp.maximum(result, -bound), bound).astype(kind)


def setup_inputs(seed: int = 0) -> dict:
    seeds = jax.random.split(jax.random.key(seed), 10)
    context = gaussian(seeds[0], (SEQ, HEADS * HEAD_DIM), 1.0, 6.0, ((0, 8), (1, 16)))
    residual = gaussian(seeds[1], (SEQ, D), 1.0, 6.0, ((0, 128),))
    o_weight = gaussian(seeds[2], (HEADS * HEAD_DIM, D), (HEADS * HEAD_DIM) ** -0.5, 0.09375, ((0, 16),))
    norm_gain = jnp.clip(1.0 + 0.18 * jax.random.normal(seeds[3], (D,), jnp.float32), 0.099609375, 1.8984375).astype(jnp.bfloat16)
    routes_keys = jax.random.split(jax.random.fold_in(seeds[4], 1), SEQ // TOK_DEV)
    routes_turns = jax.random.permutation(jax.random.fold_in(seeds[4], 3), SEQ // TOK_DEV)
    routes = jax.vmap(lambda own, number: deal_out(jax.random.fold_in(seeds[4], 2), own, number, TOK_DEV, EXPERTS, ROUTES, CAP, 2))(routes_keys, routes_turns).reshape((SEQ, ROUTES))
    gate_weights = jnp.clip(jnp.exp(math.log(0.5) - 2.3025851 * jax.random.uniform(seeds[5], (SEQ, ROUTES), jnp.float32) ** steps_of(seeds[5], (SEQ, ROUTES), ((0, 128),), -0.2, 0.2)), 0.05, 0.5)
    expert_in = gaussian(seeds[6], (EXPERTS, D, 2 * FF), D ** -0.5, 0.125, ((0, 128),))
    expert_out = gaussian(seeds[7], (EXPERTS, FF, D), FF ** -0.5, 0.21875, ((0, 128),))
    cotangent = gaussian(seeds[8], (SEQ, D), 1.0, 6.0, ((0, 128),))
    return {"context": context, "residual": residual, "o_weight": o_weight, "norm_gain": norm_gain, "routes": routes, "gate_weights": gate_weights, "expert_in": expert_in, "expert_out": expert_out, "cotangent": cotangent}


def expert_pass(item):
    arrived, grads, weight_in, weight_out = item
    hidden = weight_out.shape[0]
    gate_up = jnp.dot(arrived, weight_in, preferred_element_type=jnp.float32)
    gate_part = gate_up[:, :hidden]
    up_part = gate_up[:, hidden:]
    sigma = jax.nn.sigmoid(gate_part)
    act = (gate_part * sigma * up_part).astype(jnp.bfloat16)
    expert_y = jnp.dot(act, weight_out, preferred_element_type=jnp.float32).astype(jnp.bfloat16)
    grad_act = jnp.dot(grads, weight_out.T, preferred_element_type=jnp.float32)
    grad_gate = grad_act * up_part * sigma * (1.0 + gate_part * (1.0 - sigma))
    grad_up = grad_act * gate_part * sigma
    grad_gate_up = jnp.concatenate([grad_gate, grad_up], axis=1).astype(jnp.bfloat16)
    grad_out_w = jnp.dot(act.T, grads, preferred_element_type=jnp.float32).astype(jnp.bfloat16)
    grad_in_w = jnp.dot(arrived.T, grad_gate_up, preferred_element_type=jnp.float32).astype(jnp.bfloat16)
    grad_route = jnp.dot(grad_gate_up, weight_in.T, preferred_element_type=jnp.float32).astype(jnp.bfloat16)
    return (expert_y, grad_route, grad_in_w, grad_out_w)

def reference(context, residual, o_weight, norm_gain, routes, gate_weights, expert_in, expert_out, cotangent):
    attention = jnp.dot(context, o_weight, preferred_element_type=jnp.float32)
    mixed = (residual.astype(jnp.float32) + attention).astype(jnp.bfloat16)
    mixed_f = mixed.astype(jnp.float32)
    inv_rms = lax.rsqrt(lax.optimization_barrier(jnp.mean(mixed_f * mixed_f, axis=-1, keepdims=True)) + 1e-06)
    normed = mixed_f * inv_rms
    gain_f = norm_gain.astype(jnp.float32)
    normed_h = (normed * gain_f).astype(jnp.bfloat16)
    sources = SEQ // TOK_DEV
    per_source = TOK_DEV * ROUTES
    route_ids = routes.reshape(sources, per_source)
    expert_iota = jnp.arange(EXPERTS, dtype=jnp.int32)
    one_hot = (route_ids[:, :, None] == expert_iota[None, None, :]).astype(jnp.int32)
    route_rank = jnp.cumsum(one_hot, axis=1) - one_hot
    slot_ids = lax.optimization_barrier(jnp.sum(route_rank * one_hot, axis=-1)).astype(jnp.int32)
    source_ids = jnp.arange(sources, dtype=jnp.int32)[:, None]
    targets = (route_ids * (sources * CAP) + source_ids * CAP + slot_ids).reshape(-1).astype(jnp.int32)
    slots_all = EXPERTS * sources * CAP
    token_of = (jnp.arange(SEQ * ROUTES, dtype=jnp.int32) // ROUTES).astype(jnp.int32)
    buffer_h = jnp.zeros((slots_all, D), jnp.bfloat16).at[targets].set(normed_h[token_of])
    grad_y = (gate_weights[:, :, None] * cotangent.astype(jnp.float32)[:, None, :]).astype(jnp.bfloat16)
    buffer_g = jnp.zeros((slots_all, D), jnp.bfloat16).at[targets].set(grad_y.reshape(SEQ * ROUTES, D))
    expert_y, grad_route, d_expert_in, d_expert_out = lax.map(expert_pass, (buffer_h.reshape(EXPERTS, sources * CAP, D), buffer_g.reshape(EXPERTS, sources * CAP, D), expert_in, expert_out))
    picked = expert_y.reshape(slots_all, D)[targets].reshape(SEQ, ROUTES, D).astype(jnp.float32)
    moe_sum = lax.optimization_barrier(jnp.sum(picked * gate_weights[:, :, None], axis=1))
    layer_out = (mixed_f + moe_sum).astype(jnp.bfloat16)
    grad_back = grad_route.reshape(slots_all, D)[targets].reshape(SEQ, ROUTES, D).astype(jnp.float32)
    grad_h = lax.optimization_barrier(jnp.sum(grad_back, axis=1))
    d_gain = lax.optimization_barrier(jnp.sum(grad_h * normed, axis=0))
    grad_n = grad_h * gain_f
    inner = lax.optimization_barrier(jnp.mean(grad_n * normed, axis=-1, keepdims=True))
    d_residual = (cotangent.astype(jnp.float32) + inv_rms * (grad_n - normed * inner)).astype(jnp.bfloat16)
    d_context = jnp.dot(d_residual, o_weight.T, preferred_element_type=jnp.float32).astype(jnp.bfloat16)
    d_o_weight = jnp.dot(context.T, d_residual, preferred_element_type=jnp.float32)
    return (layer_out, d_context, d_residual, d_o_weight, d_gain, d_expert_in, d_expert_out)
```

```python
import functools

import jax
import jax.numpy as jnp
from jax import lax
from jax.experimental import pallas as pl
from jax.experimental.pallas import tpu as pltpu
from jax.sharding import PartitionSpec as P

BF = jnp.bfloat16
F32 = jnp.float32
SLOTS = 6
GROUP = 8
PACK = 3
VMEM = 56 * 1024 * 1024


def mm(a, b, da=1, db=0):
    return lax.dot_general(a, b, (((da,), (db,)), ((), ())), preferred_element_type=F32)


def contract(left_arr, right_arr, left_dim, right_dim):
    return mm(left_arr, right_arr, left_dim, right_dim)


def iota(shape, dim):
    return lax.broadcasted_iota(jnp.int32, shape, dim)


def call(body, name, out, grid, in_specs, out_specs, scratch=(), flops=0, nbytes=0):
    return pl.pallas_call(
        body,
        out_shape=out,
        grid_spec=pltpu.PrefetchScalarGridSpec(
            num_scalar_prefetch=0,
            grid=grid,
            in_specs=in_specs,
            out_specs=out_specs,
            scratch_shapes=scratch,
        ),
        compiler_params=pltpu.CompilerParams(
            dimension_semantics=("arbitrary",) * len(grid), vmem_limit_bytes=VMEM
        ),
        cost_estimate=pl.CostEstimate(flops=flops, bytes_accessed=nbytes, transcendentals=0),
        name=name,
    )


def whole(shape):
    n = len(shape)
    return pl.BlockSpec(shape, lambda i: (0,) * n)


def sds(shape, dtype):
    return jax.ShapeDtypeStruct(shape, dtype)


def slot_table(routes, n_exp):
    rows = routes.shape[0]
    lane = iota((rows, n_exp), 1)
    named = jnp.zeros((rows, n_exp), F32)
    for k in range(routes.shape[1]):
        named = named + (routes[:, k : k + 1] == lane).astype(F32)
    before = (iota((rows, rows), 0) > iota((rows, rows), 1)).astype(BF)
    rank = mm(before, named.astype(BF))
    return jnp.where(named > 0, rank, -1.0)


def gate_table(routes, gates, n_exp):
    rows = routes.shape[0]
    lane = iota((rows, n_exp), 1)
    table = jnp.zeros((rows, n_exp), F32)
    for k in range(routes.shape[1]):
        table = table + jnp.where(routes[:, k : k + 1] == lane, gates[:, k : k + 1], 0.0)
    return table


def thirds(values):
    high = values.astype(BF)
    rest = values - high.astype(F32)
    middle = rest.astype(BF)
    low = (rest - middle.astype(F32)).astype(BF)
    return high, middle, low


def pick_rows(slot, first, count):
    rows, n_exp = slot.shape
    row = iota((count, n_exp), 0) + first
    spread = (row // GROUP == iota((count, n_exp), 1)).astype(BF)
    at = mm(spread, slot.astype(BF), 1, 1)
    place = (iota((count, rows), 0) % GROUP).astype(F32)
    main = (at == place) & (place < SLOTS)
    tails = [(at == (place - SLOTS) * PACK + c) & (place >= SLOTS) for c in range(PACK)]
    return spread, main, tails


def pack_tokens(values, main, tails, quarter):
    out = []
    last = values[:, PACK * quarter :]
    for c in range(PACK):
        pick = jnp.concatenate([main.astype(BF), tails[c].astype(BF)], axis=1)
        source = jnp.concatenate([values[:, c * quarter : (c + 1) * quarter], last], axis=0)
        out.append(mm(pick, source))
    return out


def block_perm(count):
    real = count * SLOTS // GROUP
    row, col = iota((real, count), 0), iota((real, count), 1)
    owner, slot = row // SLOTS, row % SLOTS
    same = owner == col // GROUP
    place = col % GROUP
    main = same & (place == slot)
    tails = [
        same & (place == SLOTS + slot // PACK) & (slot % PACK == c) for c in range(PACK)
    ]
    return main.astype(BF), [t.astype(BF) for t in tails]


def unpack(packed, perm, quarter):
    main, tails = perm
    head = mm(main, packed).astype(BF)
    stack = jnp.concatenate([packed[:, c * quarter : (c + 1) * quarter] for c in range(PACK)], axis=0)
    tail = mm(jnp.concatenate(tails, axis=1), stack).astype(BF)
    return jnp.concatenate([head, tail], axis=1)


def repack(rows, perm, quarter):
    main, tails = perm
    last = rows[:, PACK * quarter :]
    out = []
    for c in range(PACK):
        pick = jnp.concatenate([main, tails[c]], axis=0)
        source = jnp.concatenate([rows[:, c * quarter : (c + 1) * quarter], last], axis=0)
        out.append(mm(pick, source, 0, 0).astype(BF))
    return jnp.concatenate(out, axis=1)


def pack_grads_body(n_exp, rows, routes, gates, cot, out, slot, high, middle, low):
    i = pl.program_id(0)

    @pl.when(i == 0)
    def _():
        slot[...] = slot_table(routes[...], n_exp)
        high[...], middle[...], low[...] = thirds(gate_table(routes[...], gates[...], n_exp))

    quarter = cot.shape[1] // 4
    spread, main, tails = pick_rows(slot[...], i * rows, rows)
    gate = (mm(spread, high[...], 1, 1) + mm(spread, middle[...], 1, 1)) + mm(spread, low[...], 1, 1)
    parts = pack_tokens(cot[...], main, tails, quarter)
    for c in range(PACK):
        own = jnp.sum(jnp.where(main | tails[c], gate, 0.0), axis=1, keepdims=True)
        out[:, c * quarter : (c + 1) * quarter] = (parts[c] * own).astype(BF)


def pack_grads(routes, gates, cot, n_exp):
    tok, width = cot.shape
    total, steps = n_exp * GROUP, 4
    rows = total // steps
    table = pltpu.VMEM((tok, n_exp), BF)
    return call(
        functools.partial(pack_grads_body, n_exp, rows),
        "pack_grads",
        sds((total, width * 3 // 4), BF),
        (steps,),
        [whole(routes.shape), whole(gates.shape), whole(cot.shape)],
        pl.BlockSpec((rows, width * 3 // 4), lambda i: (i, 0)),
        [pltpu.VMEM((tok, n_exp), F32), table, table, table],
        flops=2 * total * 2 * tok * width,
        nbytes=8 * total * width,
    )(routes, gates, cot)


def norm_pack_body(n_exp, rows, routes, parts, residual, gain, out, mixed_out, slot, normed_h):
    i = pl.program_id(0)

    @pl.when(i == 0)
    def _():
        slot[...] = slot_table(routes[...], n_exp)
        tok = residual.shape[0]
        step = 32

        def norm(j, carry):
            at = pl.ds(pl.multiple_of(j * step, step), step)
            total = parts[0, at, :].astype(F32)
            for b in range(1, parts.shape[0]):
                total = total + parts[b, at, :].astype(F32)
            mixed = (residual[at, :].astype(F32) + total).astype(BF)
            mixed_out[at, :] = mixed
            mixed = mixed.astype(F32)
            inv_rms = lax.rsqrt(jnp.mean(mixed * mixed, axis=-1, keepdims=True) + 1e-06)
            normed_h[at, :] = (mixed * inv_rms * gain[...].astype(F32)).astype(BF)
            return carry

        lax.fori_loop(0, tok // step, norm, 0)

    quarter = residual.shape[1] // 4
    _, main, tails = pick_rows(slot[...], i * rows, rows)
    packed = pack_tokens(normed_h[...], main, tails, quarter)
    for c in range(PACK):
        out[:, c * quarter : (c + 1) * quarter] = packed[c].astype(BF)


def norm_pack(routes, parts, residual, gain, n_exp):
    tok, width = residual.shape
    total, steps = n_exp * GROUP, 4
    rows = total // steps
    return call(
        functools.partial(norm_pack_body, n_exp, rows),
        "norm_pack",
        (sds((total, width * 3 // 4), BF), sds((tok, width), BF)),
        (steps,),
        [whole(routes.shape), whole(parts.shape), whole(residual.shape), whole(gain.shape)],
        (pl.BlockSpec((rows, width * 3 // 4), lambda i: (i, 0)), whole((tok, width))),
        [pltpu.VMEM((tok, n_exp), F32), pltpu.VMEM((tok, width), BF)],
        flops=2 * total * 2 * tok * width,
        nbytes=16 * total * width,
    )(routes, parts, residual, gain)


def pick_tokens(slot):
    rows, n_exp = slot.shape
    total = n_exp * GROUP
    spread = (iota((n_exp, total), 1) // GROUP == iota((n_exp, total), 0)).astype(BF)
    at = mm(slot.astype(BF), spread)
    place = (iota((rows, total), 1) % GROUP).astype(F32)
    main = (at == place) & (place < SLOTS)
    tails = [(at == (place - SLOTS) * PACK + c) & (place >= SLOTS) for c in range(PACK)]
    return spread, main, tails


def combine_grads_body(n_exp, routes, packed, mixed_ref, gain, cot, out, gain_out):
    tok, width = cot.shape
    quarter = width // 4
    _, main, tails = pick_tokens(slot_table(routes[...], n_exp))
    heads, last = [], jnp.zeros((tok, quarter), F32)
    for c in range(PACK):
        pick = jnp.concatenate([main.astype(BF), tails[c].astype(BF)], axis=0)
        both = mm(pick, packed[:, c * quarter : (c + 1) * quarter])
        heads.append(both[:tok])
        last = last + both[tok:]
    grad_h = jnp.concatenate(heads + [last], axis=1)
    mixed = mixed_ref[...].astype(F32)
    inv_rms = lax.rsqrt(jnp.mean(mixed * mixed, axis=-1, keepdims=True) + 1e-06)
    normed = mixed * inv_rms
    d_gain = jnp.sum(grad_h * normed, axis=0, keepdims=True)
    high, middle, low = thirds(d_gain)
    row = iota((16, width), 0)
    gain_rows = jnp.where(row == 0, high.astype(F32), 0.0)
    gain_rows = jnp.where(row == 1, middle.astype(F32), gain_rows)
    gain_rows = jnp.where(row == 2, low.astype(F32), gain_rows)
    grad_n = grad_h * gain[...].astype(F32)
    inner = jnp.mean(grad_n * normed, axis=-1, keepdims=True)
    d_res = cot[...].astype(F32) + inv_rms * (grad_n - normed * inner)
    out[0:tok, :] = d_res.astype(BF)
    out[tok : tok + 16, :] = gain_rows.astype(BF)
    gain_out[...] = d_res.astype(BF)


def combine_grads(routes, packed, mixed, gain, cot, n_exp):
    tok, width = cot.shape
    return call(
        functools.partial(combine_grads_body, n_exp),
        "combine_grads",
        (sds((tok + 16, width), BF), sds((tok, width), BF)),
        (1,),
        [whole(a.shape) for a in (routes, packed, mixed, gain, cot)],
        (whole((tok + 16, width)), whole((tok, width))),
        flops=2 * packed.shape[0] * 2 * tok * width,
        nbytes=8 * packed.shape[0] * width,
    )(routes, packed, mixed, gain, cot)


def combine_out_body(n_exp, routes, gates, packed, mixed, out):
    tok, width = mixed.shape
    quarter = width // 4
    spread, main, tails = pick_tokens(slot_table(routes[...], n_exp))
    parts = thirds(gate_table(routes[...], gates[...], n_exp))
    gate = (mm(parts[0], spread) + mm(parts[1], spread)) + mm(parts[2], spread)
    high = gate.astype(BF)
    low = (gate - high.astype(F32)).astype(BF)
    none = jnp.zeros_like(high)
    last = jnp.zeros((tok, quarter), F32)
    for c in range(PACK):
        pick = jnp.concatenate(
            [
                jnp.where(main, high, none),
                jnp.where(main, low, none),
                jnp.where(tails[c], high, none),
                jnp.where(tails[c], low, none),
            ],
            axis=0,
        )
        both = mm(pick, packed[:, c * quarter : (c + 1) * quarter])
        at = slice(c * quarter, (c + 1) * quarter)
        head = both[:tok] + both[tok : 2 * tok]
        out[:, at] = (mixed[:, at].astype(F32) + head).astype(BF)
        last = last + (both[2 * tok : 3 * tok] + both[3 * tok :])
    at = slice(PACK * quarter, width)
    out[:, at] = (mixed[:, at].astype(F32) + last).astype(BF)


def combine_out(routes, gates, packed, mixed, n_exp):
    tok, width = mixed.shape
    return call(
        functools.partial(combine_out_body, n_exp),
        "combine_out",
        sds((tok, width), BF),
        (1,),
        [whole(a.shape) for a in (routes, gates, packed, mixed)],
        whole((tok, width)),
        flops=2 * packed.shape[0] * 4 * tok * width,
        nbytes=6 * packed.shape[0] * width,
    )(routes, gates, packed, mixed)


SUB = 256


def unpack_rows(packed, quarter):
    perm = block_perm(SUB)
    return jnp.concatenate(
        [
            unpack(packed[j * SUB : (j + 1) * SUB, :], perm, quarter)
            for j in range(packed.shape[0] // SUB)
        ],
        axis=0,
    )


def repack_rows(rows, out, quarter):
    perm = block_perm(SUB)
    real = SUB * SLOTS // GROUP
    for j in range(rows.shape[0] // real):
        out[j * SUB : (j + 1) * SUB, :] = repack(rows[j * real : (j + 1) * real, :], perm, quarter)


def grad_act_body(packed, weight_out, rows_out, grad_act):
    quarter = weight_out.shape[1] // 4
    rows = unpack_rows(packed, quarter)
    rows_out[...] = rows
    grad_act[...] = mm(rows, weight_out[...], 1, 1)


def grad_act_call(packed, weight_out):
    hidden, width = weight_out.shape
    steps = 2
    block = packed.shape[0] // steps
    real = block * SLOTS // GROUP
    at = lambda i: (i, 0)
    return call(
        grad_act_body,
        "grad_act",
        (sds((real * steps, width), BF), sds((real * steps, hidden), F32)),
        (steps,),
        [pl.BlockSpec((block, packed.shape[1]), at), whole(weight_out.shape)],
        (pl.BlockSpec((real, width), at), pl.BlockSpec((real, hidden), at)),
        flops=2 * real * steps * hidden * width,
        nbytes=2 * hidden * width + 10 * real * steps * width,
    )(packed, weight_out)


def expert_body(packed, weight_in, grad_act_ref, rows_out, act_out, ggu_out, packed_out):
    width, both = weight_in.shape
    hidden = both // 2
    quarter = width // 4
    rows = unpack_rows(packed, quarter)
    rows_out[...] = rows
    gate_part = mm(rows, weight_in[:, :hidden])
    up_part = mm(rows, weight_in[:, hidden:])
    grad_act = grad_act_ref[...]
    sigma = jax.nn.sigmoid(gate_part)
    silu = gate_part * sigma
    act_out[...] = (silu * up_part).astype(BF)
    grad_gate = (grad_act * up_part * sigma * (1.0 + gate_part * (1.0 - sigma))).astype(BF)
    grad_up = (grad_act * silu).astype(BF)
    ggu_out[:, :hidden] = grad_gate
    ggu_out[:, hidden:] = grad_up
    back = mm(jnp.concatenate([grad_gate, grad_up], axis=1), weight_in[...], 1, 1).astype(BF)
    repack_rows(back, packed_out, quarter)


def expert_call(packed, weight_in, grad_act):
    width, both = weight_in.shape
    hidden = both // 2
    steps = 2
    block = packed.shape[0] // steps
    real = block * SLOTS // GROUP
    at = lambda i: (i, 0)
    return call(
        expert_body,
        "expert",
        (
            sds((real * steps, width), BF),
            sds((real * steps, hidden), BF),
            sds((real * steps, both), BF),
            sds(packed.shape, BF),
        ),
        (steps,),
        [
            pl.BlockSpec((block, packed.shape[1]), at),
            whole(weight_in.shape),
            pl.BlockSpec((real, hidden), at),
        ],
        (
            pl.BlockSpec((real, width), at),
            pl.BlockSpec((real, hidden), at),
            pl.BlockSpec((real, both), at),
            pl.BlockSpec((block, packed.shape[1]), at),
        ),
        flops=4 * real * steps * both * width,
        nbytes=2 * both * width + 10 * real * steps * width,
    )(packed, weight_in, grad_act)


def expert_y_body(act, weight_out, packed_out):
    rows = mm(act[...], weight_out[...]).astype(BF)
    repack_rows(rows, packed_out, weight_out.shape[1] // 4)


def expert_y_call(act, weight_out):
    hidden, width = weight_out.shape
    steps = 2
    real = act.shape[0] // steps
    block = real * GROUP // SLOTS
    at = lambda i: (i, 0)
    return call(
        expert_y_body,
        "expert_y",
        sds((block * steps, width * 3 // 4), BF),
        (steps,),
        [pl.BlockSpec((real, hidden), at), whole(weight_out.shape)],
        pl.BlockSpec((block, width * 3 // 4), at),
        flops=2 * real * steps * hidden * width,
        nbytes=2 * hidden * width + 4 * real * steps * width,
    )(act, weight_out)


def project_body(ctx_own, ctx_got, w_own, w_got, out):
    out[0] = (mm(ctx_own[0], w_own[...]) + mm(ctx_got[0], w_got[...])).astype(BF)


def project(ctx_own, ctx_got, w_own, w_got):
    blocks, tok, cols = ctx_own.shape
    width = w_own.shape[1]
    at = lambda i: (i, 0, 0)
    return call(
        project_body,
        "project",
        sds((blocks, tok, width), BF),
        (blocks,),
        [
            pl.BlockSpec((1, tok, cols), at),
            pl.BlockSpec((1, tok, cols), at),
            whole(w_own.shape),
            whole(w_got.shape),
        ],
        pl.BlockSpec((1, tok, width), at),
        flops=4 * blocks * tok * cols * width,
        nbytes=4 * blocks * tok * (cols + width),
    )(ctx_own, ctx_got, w_own, w_got)


def trade(values):
    n_all = lax.axis_size("ctx") * lax.axis_size("tp")
    shaped = values.reshape(n_all, GROUP, values.shape[1])
    moved = lax.all_to_all(shaped, ("ctx", "tp"), split_axis=0, concat_axis=0, tiled=True)
    return moved.reshape(values.shape)


def on_device(
    context, residual, o_weight, norm_gain, routes, gate_weights, expert_in, expert_out, cotangent
):
    tok, width = residual.shape
    n_tp = lax.axis_size("tp")
    n_ctx = lax.axis_size("ctx")
    n_exp = n_tp * n_ctx
    chips = n_tp // 2
    cols = context.shape[1]
    core = lax.axis_index("tp") % 2
    swap = [(t, t ^ 1) for t in range(n_tp)]
    same_core = [[t for t in range(n_tp) if t % 2 == c] for c in range(2)]
    gain_row = norm_gain.reshape(1, width)

    by_core = context.reshape(chips, 2, tok, cols)
    ctx_own = lax.dynamic_index_in_dim(by_core, core, 1, keepdims=False)
    ctx_give = lax.dynamic_index_in_dim(by_core, 1 - core, 1, keepdims=False)
    w_got = lax.ppermute(o_weight, "tp", swap)
    ctx_got = lax.ppermute(ctx_give, "tp", swap)
    partial = project(ctx_own, ctx_got, o_weight, w_got)
    parts = lax.all_to_all(
        partial, "tp", split_axis=0, concat_axis=0, tiled=True, axis_index_groups=same_core
    )

    grads_in = trade(pack_grads(routes, gate_weights, cotangent, n_exp))
    packed_h, mixed = norm_pack(routes, parts, residual, gain_row, n_exp)
    h_in = trade(packed_h)

    weight_in, weight_out = expert_in[0], expert_out[0]
    grads, grad_act = grad_act_call(grads_in, weight_out)
    arrived, act, ggu, packed_back = expert_call(h_in, weight_in, grad_act)
    back = trade(packed_back)
    packed_y = expert_y_call(act, weight_out)
    y_back = trade(packed_y)
    d_expert_out = contract(act, grads, 0, 0).astype(BF)[None]
    d_expert_in = contract(arrived, ggu, 0, 0).astype(BF)[None]

    d_res_gain, d_residual = combine_grads(routes, back, mixed, gain_row, cotangent, n_exp)
    layer_out = combine_out(routes, gate_weights, y_back, mixed, n_exp)

    spread = jnp.broadcast_to(d_res_gain[None], (chips,) + d_res_gain.shape)
    got = lax.all_to_all(
        spread, "tp", split_axis=0, concat_axis=0, tiled=True, axis_index_groups=same_core
    )
    d_rows = got[:, :tok].reshape(chips * tok, width)
    d_gain_chip = jnp.sum(got[:, tok : tok + 3].astype(F32), axis=(0, 1))
    flat_own = ctx_own.reshape(chips * tok, cols)
    flat_got = ctx_got.reshape(chips * tok, cols)
    w_grad_give = contract(flat_got, d_rows, 0, 0).astype(BF)
    w_grad_got = lax.ppermute(w_grad_give, "tp", swap)
    ctx_grad_give = contract(d_rows, w_got, 1, 1).astype(BF)
    ctx_grad_got = lax.ppermute(ctx_grad_give, "tp", swap)
    w_grad = (contract(flat_own, d_rows, 0, 0) + w_grad_got.astype(F32)).astype(BF)
    ctx_grad = contract(d_rows, o_weight, 1, 1).astype(BF)

    gain_got = lax.ppermute(d_gain_chip, "tp", swap)
    gain_parts = jnp.stack(thirds(d_gain_chip + gain_got)).reshape(1, -1, cols)
    gain_parts = jnp.broadcast_to(gain_parts, (n_ctx,) + gain_parts.shape[1:])
    out_cols = width // n_ctx
    by_ctx = w_grad.reshape(cols, n_ctx, out_cols).transpose(1, 0, 2)
    sent = jnp.concatenate([by_ctx, gain_parts.reshape(n_ctx, -1, out_cols)], axis=1)
    final = lax.all_to_all(sent, "ctx", split_axis=0, concat_axis=0, tiled=True).astype(F32)
    d_o_weight = jnp.sum(final[:, :cols], axis=0)
    d_gain = jnp.sum(final[:, cols:].reshape(n_ctx * 3, width), axis=0)

    mine = ctx_grad.reshape(chips, 1, tok, cols)
    other = ctx_grad_got.reshape(chips, 1, tok, cols)
    d_context = jnp.where(
        core == 0,
        jnp.concatenate([mine, other], axis=1),
        jnp.concatenate([other, mine], axis=1),
    ).reshape(context.shape)
    return (layer_out, d_context, d_residual, d_o_weight, d_gain, d_expert_in, d_expert_out)


def solution(mesh):
    rows = P(("ctx", "tp"), None)
    experts = P(("ctx", "tp"), None, None)
    in_specs = (P("ctx", "tp"), rows, P("tp", None), P(), rows, rows, experts, experts, rows)
    out_specs = (rows, P("ctx", "tp"), rows, P("tp", "ctx"), P(), experts, experts)
    return jax.shard_map(
        on_device, mesh=mesh, in_specs=in_specs, out_specs=out_specs, check_vma=False
    )
```

```python
import functools

import jax
import jax.numpy as jnp
from jax import lax
from jax.experimental import pallas as pl
from jax.experimental.pallas import tpu as pltpu
from jax.sharding import PartitionSpec as P

BF = jnp.bfloat16
F32 = jnp.float32
SLOTS = 6
GROUP = 8
PACK = 3
MIB = 1024 * 1024
BIG = ("expert", "grad_act", "expert_y", "weight_give", "weight_own", "context_grad")


def mm(a, b, da=1, db=0):
    return lax.dot_general(a, b, (((da,), (db,)), ((), ())), preferred_element_type=F32)


def contract(left_arr, right_arr, left_dim, right_dim):
    return mm(left_arr, right_arr, left_dim, right_dim)


def iota(shape, dim):
    return lax.broadcasted_iota(jnp.int32, shape, dim)


def call(body, name, out, grid, in_specs, out_specs, scratch=(), flops=0, nbytes=0):
    return pl.pallas_call(
        body,
        out_shape=out,
        grid_spec=pltpu.PrefetchScalarGridSpec(
            num_scalar_prefetch=0,
            grid=grid,
            in_specs=in_specs,
            out_specs=out_specs,
            scratch_shapes=scratch,
        ),
        compiler_params=pltpu.CompilerParams(
            dimension_semantics=("arbitrary",) * len(grid), vmem_limit_bytes=(56 if name in BIG else 26) * MIB
        ),
        cost_estimate=pl.CostEstimate(flops=flops, bytes_accessed=nbytes, transcendentals=0),
        name=name,
    )


def whole(shape):
    n = len(shape)
    return pl.BlockSpec(shape, lambda i: (0,) * n)


def sds(shape, dtype):
    return jax.ShapeDtypeStruct(shape, dtype)


def slot_table(routes, n_exp):
    rows = routes.shape[0]
    lane = iota((rows, n_exp), 1)
    named = jnp.zeros((rows, n_exp), F32)
    for k in range(routes.shape[1]):
        named = named + (routes[:, k : k + 1] == lane).astype(F32)
    before = (iota((rows, rows), 0) > iota((rows, rows), 1)).astype(BF)
    rank = mm(before, named.astype(BF))
    return jnp.where(named > 0, rank, -1.0)


def gate_table(routes, gates, n_exp):
    rows = routes.shape[0]
    lane = iota((rows, n_exp), 1)
    table = jnp.zeros((rows, n_exp), F32)
    for k in range(routes.shape[1]):
        table = table + jnp.where(routes[:, k : k + 1] == lane, gates[:, k : k + 1], 0.0)
    return table


def thirds(values):
    high = values.astype(BF)
    rest = values - high.astype(F32)
    middle = rest.astype(BF)
    low = (rest - middle.astype(F32)).astype(BF)
    return high, middle, low


def pick_rows(slot, first, count):
    rows, n_exp = slot.shape
    row = iota((count, n_exp), 0) + first
    spread = (row // GROUP == iota((count, n_exp), 1)).astype(BF)
    at = mm(spread, slot.astype(BF), 1, 1)
    place = (iota((count, rows), 0) % GROUP).astype(F32)
    main = (at == place) & (place < SLOTS)
    tails = [(at == (place - SLOTS) * PACK + c) & (place >= SLOTS) for c in range(PACK)]
    return spread, main, tails


def pack_tokens(values, main, tails, quarter):
    out = []
    last = values[:, PACK * quarter :]
    for c in range(PACK):
        pick = jnp.concatenate([main.astype(BF), tails[c].astype(BF)], axis=1)
        source = jnp.concatenate([values[:, c * quarter : (c + 1) * quarter], last], axis=0)
        out.append(mm(pick, source))
    return out


def block_perm(count):
    real = count * SLOTS // GROUP
    row, col = iota((real, count), 0), iota((real, count), 1)
    owner, slot = row // SLOTS, row % SLOTS
    same = owner == col // GROUP
    place = col % GROUP
    main = same & (place == slot)
    tails = [
        same & (place == SLOTS + slot // PACK) & (slot % PACK == c) for c in range(PACK)
    ]
    return main.astype(BF), [t.astype(BF) for t in tails]


def block_perm_back(count):
    real = count * SLOTS // GROUP
    row, col = iota((count, real), 0), iota((count, real), 1)
    place, slot = row % GROUP, col % SLOTS
    same = row // GROUP == col // SLOTS
    main = same & (place == slot)
    tails = [
        same & (place == SLOTS + slot // PACK) & (slot % PACK == c) for c in range(PACK)
    ]
    return [jnp.concatenate([main.astype(BF), t.astype(BF)], axis=1) for t in tails]


def unpack(packed, perm, quarter):
    main, tails = perm
    head = mm(main, packed).astype(BF)
    stack = jnp.concatenate([packed[:, c * quarter : (c + 1) * quarter] for c in range(PACK)], axis=0)
    tail = mm(jnp.concatenate(tails, axis=1), stack).astype(BF)
    return jnp.concatenate([head, tail], axis=1)


def repack(rows, perm, quarter):
    last = rows[:, PACK * quarter :]
    out = []
    for c in range(PACK):
        source = jnp.concatenate([rows[:, c * quarter : (c + 1) * quarter], last], axis=0)
        out.append(mm(perm[c], source).astype(BF))
    return jnp.concatenate(out, axis=1)


def pack_grads_body(n_exp, rows, routes, gates, cot, out, slot, high, middle, low):
    i = pl.program_id(0)

    @pl.when(i == 0)
    def _():
        slot[...] = slot_table(routes[...], n_exp)
        high[...], middle[...], low[...] = thirds(gate_table(routes[...], gates[...], n_exp))

    quarter = cot.shape[1] // 4
    spread, main, tails = pick_rows(slot[...], i * rows, rows)
    gate = (mm(spread, high[...], 1, 1) + mm(spread, middle[...], 1, 1)) + mm(spread, low[...], 1, 1)
    parts = pack_tokens(cot[...], main, tails, quarter)
    for c in range(PACK):
        own = jnp.sum(jnp.where(main | tails[c], gate, 0.0), axis=1, keepdims=True)
        out[:, c * quarter : (c + 1) * quarter] = (parts[c] * own).astype(BF)


def pack_grads(routes, gates, cot, n_exp):
    tok, width = cot.shape
    total, steps = n_exp * GROUP, 4
    rows = total // steps
    table = pltpu.VMEM((tok, n_exp), BF)
    return call(
        functools.partial(pack_grads_body, n_exp, rows),
        "pack_grads",
        sds((total, width * 3 // 4), BF),
        (steps,),
        [whole(routes.shape), whole(gates.shape), whole(cot.shape)],
        pl.BlockSpec((rows, width * 3 // 4), lambda i: (i, 0)),
        [pltpu.VMEM((tok, n_exp), F32), table, table, table],
        flops=2 * total * 2 * tok * width,
        nbytes=8 * total * width,
    )(routes, gates, cot)


def norm_pack_body(n_exp, rows, routes, keep_a, keep_b, *refs):
    got_a, got_b, residual, gain, out, mixed_out, slot, normed_h = (
        refs[:3], refs[3], *refs[4:]
    )
    i = pl.program_id(0)

    @pl.when(i == 0)
    def _():
        slot[...] = slot_table(routes[...], n_exp)
        tok, width = residual.shape
        step = 32

        def norm(j, carry):
            at = pl.ds(pl.multiple_of(j * step, step), step)
            left = keep_a[at, :]
            for part in got_a:
                left = left + part[at, :].astype(F32)
            right = keep_b[at, :] + got_b[at, :].astype(F32)
            total = jnp.concatenate([left, right], axis=1)
            mixed = (residual[at, :].astype(F32) + total).astype(BF)
            mixed_out[at, :] = mixed
            mixed = mixed.astype(F32)
            inv_rms = lax.rsqrt(jnp.mean(mixed * mixed, axis=-1, keepdims=True) + 1e-06)
            normed_h[at, :] = (mixed * inv_rms * gain[...].astype(F32)).astype(BF)
            return carry

        lax.fori_loop(0, tok // step, norm, 0)

    quarter = residual.shape[1] // 4
    _, main, tails = pick_rows(slot[...], i * rows, rows)
    packed = pack_tokens(normed_h[...], main, tails, quarter)
    for c in range(PACK):
        out[:, c * quarter : (c + 1) * quarter] = packed[c].astype(BF)


def norm_pack(routes, keep_a, keep_b, got_a, got_b, residual, gain, n_exp):
    tok, width = residual.shape
    total, steps = n_exp * GROUP, 4
    rows = total // steps
    args = (routes, keep_a, keep_b, *got_a, got_b, residual, gain)
    return call(
        functools.partial(norm_pack_body, n_exp, rows),
        "norm_pack",
        (sds((total, width * 3 // 4), BF), sds((tok, width), BF)),
        (steps,),
        [whole(a.shape) for a in args],
        (pl.BlockSpec((rows, width * 3 // 4), lambda i: (i, 0)), whole((tok, width))),
        [pltpu.VMEM((tok, n_exp), F32), pltpu.VMEM((tok, width), BF)],
        flops=2 * total * 2 * tok * width,
        nbytes=8 * total * width,
    )(*args)


def pick_tokens(slot):
    rows, n_exp = slot.shape
    total = n_exp * GROUP
    spread = (iota((n_exp, total), 1) // GROUP == iota((n_exp, total), 0)).astype(BF)
    at = mm(slot.astype(BF), spread)
    place = (iota((rows, total), 1) % GROUP).astype(F32)
    main = (at == place) & (place < SLOTS)
    tails = [(at == (place - SLOTS) * PACK + c) & (place >= SLOTS) for c in range(PACK)]
    return spread, main, tails


def combine_grads_body(n_exp, routes, packed, mixed_ref, gain, cot, out, res_out):
    tok, width = cot.shape
    quarter = width // 4
    _, main, tails = pick_tokens(slot_table(routes[...], n_exp))
    heads, last = [], jnp.zeros((tok, quarter), F32)
    for c in range(PACK):
        pick = jnp.concatenate([main.astype(BF), tails[c].astype(BF)], axis=0)
        both = mm(pick, packed[:, c * quarter : (c + 1) * quarter])
        heads.append(both[:tok])
        last = last + both[tok:]
    grad_h = jnp.concatenate(heads + [last], axis=1)
    mixed = mixed_ref[...].astype(F32)
    inv_rms = lax.rsqrt(jnp.mean(mixed * mixed, axis=-1, keepdims=True) + 1e-06)
    normed = mixed * inv_rms
    d_gain = jnp.sum(grad_h * normed, axis=0, keepdims=True)
    high, middle, low = thirds(d_gain)
    row = iota((16, width), 0)
    gain_rows = jnp.where(row == 0, high.astype(F32), 0.0)
    gain_rows = jnp.where(row == 1, middle.astype(F32), gain_rows)
    gain_rows = jnp.where(row == 2, low.astype(F32), gain_rows)
    grad_n = grad_h * gain[...].astype(F32)
    inner = jnp.mean(grad_n * normed, axis=-1, keepdims=True)
    d_res = cot[...].astype(F32) + inv_rms * (grad_n - normed * inner)
    d_res = d_res.astype(BF)
    gain_rows = gain_rows.astype(BF)
    res_out[...] = d_res
    for h, at in enumerate((slice(0, width // 2), slice(width // 2, width))):
        out[h, 0:tok, :] = d_res[:, at]
        out[h, tok : tok + 16, :] = gain_rows[:, at]


def combine_grads(routes, packed, mixed, gain, cot, n_exp):
    tok, width = cot.shape
    return call(
        functools.partial(combine_grads_body, n_exp),
        "combine_grads",
        (sds((2, tok + 16, width // 2), BF), sds((tok, width), BF)),
        (1,),
        [whole(a.shape) for a in (routes, packed, mixed, gain, cot)],
        (whole((2, tok + 16, width // 2)), whole((tok, width))),
        flops=2 * packed.shape[0] * 2 * tok * width,
        nbytes=8 * packed.shape[0] * width,
    )(routes, packed, mixed, gain, cot)


def combine_out_body(n_exp, routes, gates, packed, mixed, out):
    tok, width = mixed.shape
    quarter = width // 4
    spread, main, tails = pick_tokens(slot_table(routes[...], n_exp))
    parts = thirds(gate_table(routes[...], gates[...], n_exp))
    gate = (mm(parts[0], spread) + mm(parts[1], spread)) + mm(parts[2], spread)
    high = gate.astype(BF)
    low = (gate - high.astype(F32)).astype(BF)
    none = jnp.zeros_like(high)
    last = jnp.zeros((tok, quarter), F32)
    for c in range(PACK):
        pick = jnp.concatenate(
            [
                jnp.where(main, high, none),
                jnp.where(main, low, none),
                jnp.where(tails[c], high, none),
                jnp.where(tails[c], low, none),
            ],
            axis=0,
        )
        both = mm(pick, packed[:, c * quarter : (c + 1) * quarter])
        at = slice(c * quarter, (c + 1) * quarter)
        head = both[:tok] + both[tok : 2 * tok]
        out[:, at] = (mixed[:, at].astype(F32) + head).astype(BF)
        last = last + (both[2 * tok : 3 * tok] + both[3 * tok :])
    at = slice(PACK * quarter, width)
    out[:, at] = (mixed[:, at].astype(F32) + last).astype(BF)


def combine_out(routes, gates, packed, mixed, n_exp):
    tok, width = mixed.shape
    return call(
        functools.partial(combine_out_body, n_exp),
        "combine_out",
        sds((tok, width), BF),
        (1,),
        [whole(a.shape) for a in (routes, gates, packed, mixed)],
        whole((tok, width)),
        flops=2 * packed.shape[0] * 4 * tok * width,
        nbytes=6 * packed.shape[0] * width,
    )(routes, gates, packed, mixed)


SUB = 256


def unpack_rows(packed, quarter):
    perm = block_perm(SUB)
    return jnp.concatenate(
        [
            unpack(packed[j * SUB : (j + 1) * SUB, :], perm, quarter)
            for j in range(packed.shape[0] // SUB)
        ],
        axis=0,
    )


def repack_rows(rows, out, quarter):
    perm = block_perm_back(SUB)
    real = SUB * SLOTS // GROUP
    for j in range(rows.shape[0] // real):
        out[j * SUB : (j + 1) * SUB, :] = repack(rows[j * real : (j + 1) * real, :], perm, quarter)


def grad_act_body(packed, weight_out, rows_out, grad_act):
    quarter = weight_out.shape[1] // 4
    rows = unpack_rows(packed, quarter)
    rows_out[...] = rows
    grad_act[...] = mm(rows, weight_out[...], 1, 1)


def grad_act_call(packed, weight_out):
    hidden, width = weight_out.shape
    steps = 2
    block = packed.shape[0] // steps
    real = block * SLOTS // GROUP
    at = lambda i: (i, 0)
    return call(
        grad_act_body,
        "grad_act",
        (sds((real * steps, width), BF), sds((real * steps, hidden), F32)),
        (steps,),
        [pl.BlockSpec((block, packed.shape[1]), at), whole(weight_out.shape)],
        (pl.BlockSpec((real, width), at), pl.BlockSpec((real, hidden), at)),
        flops=2 * real * steps * hidden * width,
        nbytes=2 * hidden * width + 10 * real * steps * width,
    )(packed, weight_out)


def expert_body(packed, weight_in, grad_act_ref, rows_out, act_out, ggu_out, packed_out):
    width, both = weight_in.shape
    hidden = both // 2
    quarter = width // 4
    rows = unpack_rows(packed, quarter)
    rows_out[...] = rows
    gate_part = mm(rows, weight_in[:, :hidden])
    up_part = mm(rows, weight_in[:, hidden:])
    grad_act = grad_act_ref[...]
    sigma = jax.nn.sigmoid(gate_part)
    silu = gate_part * sigma
    act_out[...] = (silu * up_part).astype(BF)
    grad_gate = (grad_act * up_part * sigma * (1.0 + gate_part * (1.0 - sigma))).astype(BF)
    grad_up = (grad_act * silu).astype(BF)
    ggu_out[:, :hidden] = grad_gate
    ggu_out[:, hidden:] = grad_up
    back = mm(jnp.concatenate([grad_gate, grad_up], axis=1), weight_in[...], 1, 1).astype(BF)
    repack_rows(back, packed_out, quarter)


def expert_call(packed, weight_in, grad_act):
    width, both = weight_in.shape
    hidden = both // 2
    steps = 2
    block = packed.shape[0] // steps
    real = block * SLOTS // GROUP
    at = lambda i: (i, 0)
    return call(
        expert_body,
        "expert",
        (
            sds((real * steps, width), BF),
            sds((real * steps, hidden), BF),
            sds((real * steps, both), BF),
            sds(packed.shape, BF),
        ),
        (steps,),
        [
            pl.BlockSpec((block, packed.shape[1]), at),
            whole(weight_in.shape),
            pl.BlockSpec((real, hidden), at),
        ],
        (
            pl.BlockSpec((real, width), at),
            pl.BlockSpec((real, hidden), at),
            pl.BlockSpec((real, both), at),
            pl.BlockSpec((block, packed.shape[1]), at),
        ),
        flops=4 * real * steps * both * width,
        nbytes=2 * both * width + 10 * real * steps * width,
    )(packed, weight_in, grad_act)


def expert_y_body(act, weight_out, packed_out):
    rows = mm(act[...], weight_out[...]).astype(BF)
    repack_rows(rows, packed_out, weight_out.shape[1] // 4)


def expert_y_call(act, weight_out):
    hidden, width = weight_out.shape
    steps = 2
    real = act.shape[0] // steps
    block = real * GROUP // SLOTS
    at = lambda i: (i, 0)
    return call(
        expert_y_body,
        "expert_y",
        sds((block * steps, width * 3 // 4), BF),
        (steps,),
        [pl.BlockSpec((real, hidden), at), whole(weight_out.shape)],
        pl.BlockSpec((block, width * 3 // 4), at),
        flops=2 * real * steps * hidden * width,
        nbytes=2 * hidden * width + 4 * real * steps * width,
    )(act, weight_out)


def rows_of(ref, order, places):
    return jnp.concatenate([ref[order[p]] for p in places], axis=0)


def product(order, places, ctx_own, ctx_got, w_own, w_got, cols):
    own = mm(rows_of(ctx_own, order, places), w_own[:, cols])
    return own + mm(rows_of(ctx_got, order, places), w_got[:, cols])


def halves(w):
    half = w.shape[1] // 2
    return slice(0, half), slice(half, 2 * half)


def project_first_body(order, ctx_own, ctx_got, w_own, w_got, over_z, *over_x):
    left, right = halves(w_own)
    args = (ctx_own, ctx_got, w_own, w_got)
    over_z[...] = product(order, [1, 3, 5, 7], *args, left).astype(BF)
    for d in range(3):
        over_x[d][...] = product(order, [2 * d + 2, 2 * d + 3], *args, right).astype(BF)


def project_keep_body(order, ctx_own, ctx_got, w_own, w_got, keep_a, keep_b):
    left, right = halves(w_own)
    args = (ctx_own, ctx_got, w_own, w_got)
    keep_b[...] = product(order, [0, 1], *args, right)
    keep_a[...] = product(order, [0, 2, 4, 6], *args, left)


def add_body(order, kept_a, kept_b, got_z, got_1, got_2, got_3, keep_a, keep_b, over_z, *over_x):
    tok = keep_a.shape[0]
    keep_a[...] = kept_a[0:tok, :] + got_z[0:tok, :].astype(F32)
    for d in range(3):
        at = slice((d + 1) * tok, (d + 2) * tok)
        over_x[d][...] = (kept_a[at, :] + got_z[at, :].astype(F32)).astype(BF)
    total = kept_b[...]
    for got in (got_1, got_2, got_3):
        total = total + got[...].astype(F32)
    keep_b[...] = total[:tok]
    over_z[...] = total[tok:].astype(BF)


def plain(body, name, outs, order, *args, flops=0, scratch=()):
    nbytes = sum(a.size * a.dtype.itemsize for a in args)
    nbytes += sum(o.size * o.dtype.itemsize for o in outs)
    return call(
        body,
        name,
        tuple(outs),
        (1,),
        [pl.BlockSpec(memory_space=pltpu.SMEM)] + [whole(a.shape) for a in args],
        tuple(whole(o.shape) for o in outs),
        scratch,
        flops=flops,
        nbytes=nbytes,
    )(order, *args)


N_BLOCKS = 11


def gather_parts(blocks, first, last):
    same_z, other_z, left_z, right_z = blocks[:4], blocks[4], blocks[5:8], blocks[8:]
    left, right = [], []
    for d in range(4):
        left += [same_z[d][0, first:last, :]]
        left += [left_z[d - 1][first:last, :] if d else other_z[0, first:last, :]]
        right += [same_z[d][1, first:last, :]]
        right += [right_z[d - 1][first:last, :] if d else other_z[1, first:last, :]]
    return left, right


def gather_rows(blocks):
    left, right = gather_parts(blocks, 0, blocks[0].shape[1] - 16)
    return jnp.concatenate(left, axis=0), jnp.concatenate(right, axis=0)


def weight_give_body(order, ctx_got, *refs):
    blocks, (give, gain_out) = refs[:N_BLOCKS], refs[N_BLOCKS:]
    tok = ctx_got.shape[1]
    ctx = rows_of(ctx_got, order, range(8))
    half = blocks[0].shape[2]
    gains = gather_parts(blocks, tok, tok + 16)
    for h, rows in enumerate(gather_rows(blocks)):
        give[:, h * half : (h + 1) * half] = mm(ctx, rows, 0, 0).astype(BF)
        total = jnp.zeros((16, half), F32)
        for part in gains[h]:
            total = total + part.astype(F32)
        total = jnp.sum(total, axis=0, keepdims=True)
        gain_out[:, h * half : (h + 1) * half] = jnp.broadcast_to(total, (8, half))


def context_grad_body(order, w_own, w_got, *refs):
    blocks, (own, give) = refs[:N_BLOCKS], refs[N_BLOCKS:]
    tok = own.shape[1]
    half = blocks[0].shape[2]
    left, right = gather_rows(blocks)
    for w, out in ((w_got, give), (w_own, own)):
        grad = mm(left, w[:, :half], 1, 1) + mm(right, w[:, half:], 1, 1)
        grad = grad.astype(BF)
        for p in range(8):
            out[order[p] // 2] = grad[p * tok : (p + 1) * tok]


def weight_own_body(order, ctx_own, got, gain_own, gain_got, *refs):
    blocks, outs, held = refs[:N_BLOCKS], refs[N_BLOCKS:-1], refs[-1]
    cols = ctx_own.shape[2]
    n_ctx, _, width = held.shape
    ctx = rows_of(ctx_own, order, range(8))
    half = blocks[0].shape[2]
    parts = thirds(gain_own[0:1, :] + gain_got[0:1, :])
    row = iota((32, width), 0)
    gain = jnp.zeros((32, width), F32)
    for p in range(3):
        for j in range(n_ctx):
            piece = parts[p][:, j * width : (j + 1) * width].astype(F32)
            gain = jnp.where(row == p * n_ctx + j, piece, gain)
    gain = gain.astype(BF)
    per_half = half // width
    for h, rows in enumerate(gather_rows(blocks)):
        grad = mm(ctx, rows, 0, 0) + got[:, h * half : (h + 1) * half].astype(F32)
        grad = grad.astype(BF)
        for j in range(per_half):
            held[h * per_half + j, 0:cols, :] = grad[:, j * width : (j + 1) * width]
            held[h * per_half + j, cols : cols + 32, :] = gain
    for d, out in enumerate(outs):
        out[...] = held[(order[8] + d) % n_ctx]


def trade(values):
    n_all = lax.axis_size("ctx") * lax.axis_size("tp")
    shaped = values.reshape(n_all, GROUP, values.shape[1])
    moved = lax.all_to_all(shaped, ("ctx", "tp"), split_axis=0, concat_axis=0, tiled=True)
    return moved.reshape(values.shape)


def on_device(
    context, residual, o_weight, norm_gain, routes, gate_weights, expert_in, expert_out, cotangent
):
    tok, width = residual.shape
    n_tp = lax.axis_size("tp")
    n_ctx = lax.axis_size("ctx")
    n_exp = n_tp * n_ctx
    chips = n_tp // 2
    cols = context.shape[1]
    core = lax.axis_index("tp") % 2
    gain_row = norm_gain.reshape(1, width)

    t = lax.axis_index("tp")
    x, z = t // 4, t // 2 % 2
    pairs = [(d, o) for d in range(4) for o in range(2)]
    order = jnp.stack([(x + d) % 4 * 4 + (z ^ o) * 2 + core for d, o in pairs])
    came = jnp.stack([(x - d) % 4 * 4 + (z ^ o) * 2 + core for d, o in pairs])

    def over_x(d):
        return [(u, (u + 4 * d) % n_tp) for u in range(n_tp)]

    over_z = [(u, u ^ 2) for u in range(n_tp)]
    swap = [(u, u ^ 1) for u in range(n_tp)]

    def move(values, perm):
        return lax.ppermute(values, "tp", perm)

    ctx_own = context.reshape(n_tp, tok, cols)
    ctx_got = move(ctx_own, swap)
    w_got = move(o_weight, swap)
    packed_g = pack_grads(routes, gate_weights, cotangent, n_exp)
    packed_g, ctx_got = lax.optimization_barrier((packed_g, ctx_got))
    grads_in = trade(packed_g)
    half = width // 2
    operands = (ctx_own, ctx_got, o_weight, w_got)
    per_block = 4 * tok * cols * half
    send_z, *send_x = plain(
        project_first_body,
        "project_first",
        [sds((4 * tok, half), BF)] + [sds((2 * tok, half), BF)] * 3,
        order,
        *operands,
        flops=10 * per_block,
    )
    got_z = move(send_z, over_z)
    got_x = [move(send_x[d], over_x(d + 1)) for d in range(3)]
    kept_a, kept_b = plain(
        project_keep_body,
        "project_keep",
        [sds((4 * tok, half), F32), sds((2 * tok, half), F32)],
        order,
        *operands,
        flops=6 * per_block,
    )
    keep_a, keep_b, send_b, *send_a = plain(
        add_body,
        "add",
        [sds((tok, half), F32)] * 2 + [sds((tok, half), BF)] * 4,
        order,
        kept_a,
        kept_b,
        got_z,
        *got_x,
    )
    got_a = [move(send_a[d], over_x(d + 1)) for d in range(3)]
    got_b = move(send_b, over_z)

    packed_h, mixed = norm_pack(
        routes, keep_a, keep_b, got_a, got_b, residual, gain_row, n_exp
    )
    h_in = trade(packed_h)

    weight_in, weight_out = expert_in[0], expert_out[0]
    grads, grad_act = grad_act_call(grads_in, weight_out)
    arrived, act, ggu, packed_back = expert_call(h_in, weight_in, grad_act)
    back = trade(packed_back)
    packed_y = expert_y_call(act, weight_out)
    d_expert_out = contract(act, grads, 0, 0).astype(BF)[None]
    d_expert_in = contract(arrived, ggu, 0, 0).astype(BF)[None]
    back, packed_y, d_expert_out, d_expert_in = lax.optimization_barrier(
        (back, packed_y, d_expert_out, d_expert_in)
    )
    res, d_residual = combine_grads(routes, back, mixed, gain_row, cotangent, n_exp)

    same_z = [res] + [move(res, over_x(d)) for d in range(1, 4)]
    other_z = move(res, over_z)
    left_z = [move(v[0], over_z) for v in same_z[1:]]
    right_z = [move(other_z[1], over_x(d)) for d in range(1, 4)]
    blocks = [*same_z, other_z, *left_z, *right_z]
    packed_y, *blocks = lax.optimization_barrier((packed_y, *blocks))
    y_back = trade(packed_y)

    w_give, gain_own = plain(
        weight_give_body,
        "weight_give",
        [sds((cols, width), BF), sds((8, width), F32)],
        came,
        ctx_got,
        *blocks,
        flops=16 * tok * cols * width,
    )
    w_grad_got = move(w_give, swap)
    gain_got = move(gain_own, swap)
    out_cols = width // n_ctx
    part = (cols + 32, out_cols)
    sent = plain(
        weight_own_body,
        "weight_own",
        [sds(part, BF)] * n_ctx,
        jnp.concatenate([came, lax.axis_index("ctx").reshape(1)]),
        ctx_own,
        w_grad_got,
        gain_own,
        gain_got,
        *blocks,
        flops=16 * tok * cols * width,
        scratch=[pltpu.VMEM((n_ctx,) + part, BF)],
    )
    w_after, *sent = lax.optimization_barrier((o_weight, *sent))
    ctx_mine, ctx_grad_give = plain(
        context_grad_body,
        "context_grad",
        [sds((chips, tok, cols), BF)] * 2,
        came,
        w_after,
        w_got,
        *blocks,
        flops=32 * tok * cols * width,
    )
    ctx_other = move(ctx_grad_give, swap)
    final = [sent[0]]
    for d in range(1, n_ctx):
        around = [(u, (u + d) % n_ctx) for u in range(n_ctx)]
        final.append(lax.ppermute(sent[d], "ctx", around))
    layer_out = combine_out(routes, gate_weights, y_back, mixed, n_exp)
    layer_out, *final = lax.optimization_barrier((layer_out, *final))
    final = sum(f.astype(F32) for f in final)
    d_o_weight = final[:cols]
    d_gain = jnp.sum(final[cols : cols + 3 * n_ctx].reshape(3, width), axis=0)

    mine = ctx_mine.reshape(chips, 1, tok, cols)
    other = ctx_other.reshape(chips, 1, tok, cols)
    d_context = jnp.where(
        core == 0,
        jnp.concatenate([mine, other], axis=1),
        jnp.concatenate([other, mine], axis=1),
    ).reshape(context.shape)
    return (layer_out, d_context, d_residual, d_o_weight, d_gain, d_expert_in, d_expert_out)


def solution(mesh):
    rows = P(("ctx", "tp"), None)
    experts = P(("ctx", "tp"), None, None)
    in_specs = (P("ctx", "tp"), rows, P("tp", None), P(), rows, rows, experts, experts, rows)
    out_specs = (rows, P("ctx", "tp"), rows, P("tp", "ctx"), P(), experts, experts)
    return jax.shard_map(
        on_device, mesh=mesh, in_specs=in_specs, out_specs=out_specs, check_vma=False
    )
```

```python
import functools

import jax
import jax.numpy as jnp
from jax import lax
from jax.experimental import pallas as pl
from jax.experimental.pallas import tpu as pltpu
from jax.sharding import PartitionSpec as P

BF = jnp.bfloat16
F32 = jnp.float32
SLOTS = 6
GROUP = 8
PACK = 3
MIB = 1024 * 1024
BIG = ("expert", "expert_y", "weight_give", "weight_own", "context_grad")


def mm(a, b, da=1, db=0):
    return lax.dot_general(a, b, (((da,), (db,)), ((), ())), preferred_element_type=F32)


def contract(left_arr, right_arr, left_dim, right_dim):
    return mm(left_arr, right_arr, left_dim, right_dim)


def iota(shape, dim):
    return lax.broadcasted_iota(jnp.int32, shape, dim)


def call(body, name, out, grid, in_specs, out_specs, scratch=(), flops=0, nbytes=0):
    return pl.pallas_call(
        body,
        out_shape=out,
        grid_spec=pltpu.PrefetchScalarGridSpec(
            num_scalar_prefetch=0,
            grid=grid,
            in_specs=in_specs,
            out_specs=out_specs,
            scratch_shapes=scratch,
        ),
        compiler_params=pltpu.CompilerParams(
            dimension_semantics=("arbitrary",) * len(grid), vmem_limit_bytes=(56 if name in BIG else 26) * MIB
        ),
        cost_estimate=pl.CostEstimate(flops=flops, bytes_accessed=nbytes, transcendentals=0),
        name=name,
    )


def whole(shape):
    n = len(shape)
    return pl.BlockSpec(shape, lambda i: (0,) * n)


def sds(shape, dtype):
    return jax.ShapeDtypeStruct(shape, dtype)


def slot_table(routes, n_exp):
    rows = routes.shape[0]
    lane = iota((rows, n_exp), 1)
    named = jnp.zeros((rows, n_exp), F32)
    for k in range(routes.shape[1]):
        named = named + (routes[:, k : k + 1] == lane).astype(F32)
    before = (iota((rows, rows), 0) > iota((rows, rows), 1)).astype(BF)
    rank = mm(before, named.astype(BF))
    return jnp.where(named > 0, rank, -1.0)


def gate_table(routes, gates, n_exp):
    rows = routes.shape[0]
    lane = iota((rows, n_exp), 1)
    table = jnp.zeros((rows, n_exp), F32)
    for k in range(routes.shape[1]):
        table = table + jnp.where(routes[:, k : k + 1] == lane, gates[:, k : k + 1], 0.0)
    return table


def thirds(values):
    high = values.astype(BF)
    rest = values - high.astype(F32)
    middle = rest.astype(BF)
    low = (rest - middle.astype(F32)).astype(BF)
    return high, middle, low


def pick_rows(slot, first, count):
    rows, n_exp = slot.shape
    row = iota((count, n_exp), 0) + first
    spread = (row // GROUP == iota((count, n_exp), 1)).astype(BF)
    at = mm(spread, slot.astype(BF), 1, 1)
    place = (iota((count, rows), 0) % GROUP).astype(F32)
    main = (at == place) & (place < SLOTS)
    tails = [(at == (place - SLOTS) * PACK + c) & (place >= SLOTS) for c in range(PACK)]
    return spread, main, tails


def pack_tokens(values, main, tails, quarter):
    out = []
    last = values[:, PACK * quarter :]
    for c in range(PACK):
        pick = jnp.concatenate([main.astype(BF), tails[c].astype(BF)], axis=1)
        source = jnp.concatenate([values[:, c * quarter : (c + 1) * quarter], last], axis=0)
        out.append(mm(pick, source))
    return out


def block_perm(count):
    real = count * SLOTS // GROUP
    row, col = iota((real, count), 0), iota((real, count), 1)
    owner, slot = row // SLOTS, row % SLOTS
    same = owner == col // GROUP
    place = col % GROUP
    main = same & (place == slot)
    tails = [
        same & (place == SLOTS + slot // PACK) & (slot % PACK == c) for c in range(PACK)
    ]
    return main.astype(BF), [t.astype(BF) for t in tails]


def block_perm_back(count):
    real = count * SLOTS // GROUP
    row, col = iota((count, real), 0), iota((count, real), 1)
    place, slot = row % GROUP, col % SLOTS
    same = row // GROUP == col // SLOTS
    main = same & (place == slot)
    tails = [
        same & (place == SLOTS + slot // PACK) & (slot % PACK == c) for c in range(PACK)
    ]
    return [jnp.concatenate([main.astype(BF), t.astype(BF)], axis=1) for t in tails]


def unpack(packed, perm, quarter):
    main, tails = perm
    head = mm(main, packed).astype(BF)
    stack = jnp.concatenate([packed[:, c * quarter : (c + 1) * quarter] for c in range(PACK)], axis=0)
    tail = mm(jnp.concatenate(tails, axis=1), stack).astype(BF)
    return jnp.concatenate([head, tail], axis=1)


def repack(rows, perm, quarter):
    last = rows[:, PACK * quarter :]
    out = []
    for c in range(PACK):
        source = jnp.concatenate([rows[:, c * quarter : (c + 1) * quarter], last], axis=0)
        out.append(mm(perm[c], source).astype(BF))
    return jnp.concatenate(out, axis=1)


def pack_grads_body(n_exp, rows, routes, gates, cot, out, slot, high, middle, low):
    i = pl.program_id(0)

    @pl.when(i == 0)
    def _():
        slot[...] = slot_table(routes[...], n_exp)
        high[...], middle[...], low[...] = thirds(gate_table(routes[...], gates[...], n_exp))

    quarter = cot.shape[1] // 4
    spread, main, tails = pick_rows(slot[...], i * rows, rows)
    gate = (mm(spread, high[...], 1, 1) + mm(spread, middle[...], 1, 1)) + mm(spread, low[...], 1, 1)
    parts = pack_tokens(cot[...], main, tails, quarter)
    for c in range(PACK):
        own = jnp.sum(jnp.where(main | tails[c], gate, 0.0), axis=1, keepdims=True)
        out[:, c * quarter : (c + 1) * quarter] = (parts[c] * own).astype(BF)


def pack_grads(routes, gates, cot, n_exp):
    tok, width = cot.shape
    total, steps = n_exp * GROUP, 4
    rows = total // steps
    table = pltpu.VMEM((tok, n_exp), BF)
    return call(
        functools.partial(pack_grads_body, n_exp, rows),
        "pack_grads",
        sds((total, width * 3 // 4), BF),
        (steps,),
        [whole(routes.shape), whole(gates.shape), whole(cot.shape)],
        pl.BlockSpec((rows, width * 3 // 4), lambda i: (i, 0)),
        [pltpu.VMEM((tok, n_exp), F32), table, table, table],
        flops=2 * total * 2 * tok * width,
        nbytes=8 * total * width,
    )(routes, gates, cot)


def norm_pack_body(n_exp, rows, routes, keep_a, keep_b, *refs):
    got_a, got_b, residual, gain, packed_g, out, mixed_out, slot, normed_h = (
        refs[:3], refs[3], *refs[4:]
    )
    i = pl.program_id(0)

    @pl.when(i == 0)
    def _():
        slot[...] = slot_table(routes[...], n_exp)
        tok, width = residual.shape
        step = 32

        def norm(j, carry):
            at = pl.ds(pl.multiple_of(j * step, step), step)
            left = keep_a[at, :]
            for part in got_a:
                left = left + part[at, :].astype(F32)
            right = keep_b[at, :] + got_b[at, :].astype(F32)
            total = jnp.concatenate([left, right], axis=1)
            mixed = (residual[at, :].astype(F32) + total).astype(BF)
            mixed_out[at, :] = mixed
            mixed = mixed.astype(F32)
            inv_rms = lax.rsqrt(jnp.mean(mixed * mixed, axis=-1, keepdims=True) + 1e-06)
            normed_h[at, :] = (mixed * inv_rms * gain[...].astype(F32)).astype(BF)
            return carry

        lax.fori_loop(0, tok // step, norm, 0)

    quarter = residual.shape[1] // 4
    _, main, tails = pick_rows(slot[...], i * rows, rows)
    packed = pack_tokens(normed_h[...], main, tails, quarter)
    for c in range(PACK):
        out[:, c * quarter : (c + 1) * quarter] = packed[c].astype(BF)
    out[:, PACK * quarter :] = packed_g[...]


def norm_pack(routes, keep_a, keep_b, got_a, got_b, residual, gain, packed_g, n_exp):
    tok, width = residual.shape
    total, steps = n_exp * GROUP, 4
    rows = total // steps
    args = (routes, keep_a, keep_b, *got_a, got_b, residual, gain)
    return call(
        functools.partial(norm_pack_body, n_exp, rows),
        "norm_pack",
        (sds((total, width * 3 // 2), BF), sds((tok, width), BF)),
        (steps,),
        [whole(a.shape) for a in args] + [pl.BlockSpec((rows, width * 3 // 4), lambda i: (i, 0))],
        (pl.BlockSpec((rows, width * 3 // 2), lambda i: (i, 0)), whole((tok, width))),
        [pltpu.VMEM((tok, n_exp), F32), pltpu.VMEM((tok, width), BF)],
        flops=2 * total * 2 * tok * width,
        nbytes=8 * total * width,
    )(*args, packed_g)


def pick_tokens(slot):
    rows, n_exp = slot.shape
    total = n_exp * GROUP
    spread = (iota((n_exp, total), 1) // GROUP == iota((n_exp, total), 0)).astype(BF)
    at = mm(slot.astype(BF), spread)
    place = (iota((rows, total), 1) % GROUP).astype(F32)
    main = (at == place) & (place < SLOTS)
    tails = [(at == (place - SLOTS) * PACK + c) & (place >= SLOTS) for c in range(PACK)]
    return spread, main, tails


def combine_grads_body(n_exp, routes, packed, mixed_ref, gain, cot, out, res_out):
    tok, width = cot.shape
    quarter = width // 4
    _, main, tails = pick_tokens(slot_table(routes[...], n_exp))
    heads, last = [], jnp.zeros((tok, quarter), F32)
    for c in range(PACK):
        pick = jnp.concatenate([main.astype(BF), tails[c].astype(BF)], axis=0)
        both = mm(pick, packed[:, c * quarter : (c + 1) * quarter])
        heads.append(both[:tok])
        last = last + both[tok:]
    grad_h = jnp.concatenate(heads + [last], axis=1)
    mixed = mixed_ref[...].astype(F32)
    inv_rms = lax.rsqrt(jnp.mean(mixed * mixed, axis=-1, keepdims=True) + 1e-06)
    normed = mixed * inv_rms
    d_gain = jnp.sum(grad_h * normed, axis=0, keepdims=True)
    high, middle, low = thirds(d_gain)
    row = iota((16, width), 0)
    gain_rows = jnp.where(row == 0, high.astype(F32), 0.0)
    gain_rows = jnp.where(row == 1, middle.astype(F32), gain_rows)
    gain_rows = jnp.where(row == 2, low.astype(F32), gain_rows)
    grad_n = grad_h * gain[...].astype(F32)
    inner = jnp.mean(grad_n * normed, axis=-1, keepdims=True)
    d_res = cot[...].astype(F32) + inv_rms * (grad_n - normed * inner)
    d_res = d_res.astype(BF)
    gain_rows = gain_rows.astype(BF)
    res_out[...] = d_res
    out[0:tok, :] = d_res
    out[tok : tok + 16, :] = gain_rows


def combine_grads(routes, packed, mixed, gain, cot, n_exp):
    tok, width = cot.shape
    return call(
        functools.partial(combine_grads_body, n_exp),
        "combine_grads",
        (sds((tok + 16, width), BF), sds((tok, width), BF)),
        (1,),
        [whole(a.shape) for a in (routes, packed, mixed, gain, cot)],
        (whole((tok + 16, width)), whole((tok, width))),
        flops=2 * packed.shape[0] * 2 * tok * width,
        nbytes=8 * packed.shape[0] * width,
    )(routes, packed, mixed, gain, cot)


def combine_out_body(n_exp, routes, gates, packed, mixed, out):
    tok, width = mixed.shape
    quarter = width // 4
    spread, main, tails = pick_tokens(slot_table(routes[...], n_exp))
    parts = thirds(gate_table(routes[...], gates[...], n_exp))
    gate = (mm(parts[0], spread) + mm(parts[1], spread)) + mm(parts[2], spread)
    high = gate.astype(BF)
    low = (gate - high.astype(F32)).astype(BF)
    none = jnp.zeros_like(high)
    last = jnp.zeros((tok, quarter), F32)
    for c in range(PACK):
        pick = jnp.concatenate(
            [
                jnp.where(main, high, none),
                jnp.where(main, low, none),
                jnp.where(tails[c], high, none),
                jnp.where(tails[c], low, none),
            ],
            axis=0,
        )
        both = mm(pick, packed[:, c * quarter : (c + 1) * quarter])
        at = slice(c * quarter, (c + 1) * quarter)
        head = both[:tok] + both[tok : 2 * tok]
        out[:, at] = (mixed[:, at].astype(F32) + head).astype(BF)
        last = last + (both[2 * tok : 3 * tok] + both[3 * tok :])
    at = slice(PACK * quarter, width)
    out[:, at] = (mixed[:, at].astype(F32) + last).astype(BF)


def combine_out(routes, gates, packed, mixed, n_exp):
    tok, width = mixed.shape
    return call(
        functools.partial(combine_out_body, n_exp),
        "combine_out",
        sds((tok, width), BF),
        (1,),
        [whole(a.shape) for a in (routes, gates, packed, mixed)],
        whole((tok, width)),
        flops=2 * packed.shape[0] * 4 * tok * width,
        nbytes=6 * packed.shape[0] * width,
    )(routes, gates, packed, mixed)


SUB = 256


def unpack_rows(packed, quarter):
    perm = block_perm(SUB)
    return jnp.concatenate(
        [
            unpack(packed[j * SUB : (j + 1) * SUB, :], perm, quarter)
            for j in range(packed.shape[0] // SUB)
        ],
        axis=0,
    )


def repack_rows(rows, out, quarter):
    perm = block_perm_back(SUB)
    real = SUB * SLOTS // GROUP
    for j in range(rows.shape[0] // real):
        out[j * SUB : (j + 1) * SUB, :] = repack(rows[j * real : (j + 1) * real, :], perm, quarter)


def expert_body(
    packed_h, packed_g, weight_in, weight_out, rows_out, grads_out, act_out, ggu_out, packed_out
):
    width, both = weight_in.shape
    hidden = both // 2
    quarter = width // 4
    rows = unpack_rows(packed_h, quarter)
    rows_out[...] = rows
    gate_part = mm(rows, weight_in[:, :hidden])
    up_part = mm(rows, weight_in[:, hidden:])
    sigma = jax.nn.sigmoid(gate_part)
    silu = gate_part * sigma
    act_out[...] = (silu * up_part).astype(BF)
    grads = unpack_rows(packed_g, quarter)
    grads_out[...] = grads
    grad_act = mm(grads, weight_out[...], 1, 1)
    grad_gate = (grad_act * up_part * sigma * (1.0 + gate_part * (1.0 - sigma))).astype(BF)
    grad_up = (grad_act * silu).astype(BF)
    ggu_out[:, :hidden] = grad_gate
    ggu_out[:, hidden:] = grad_up
    back = mm(jnp.concatenate([grad_gate, grad_up], axis=1), weight_in[...], 1, 1).astype(BF)
    repack_rows(back, packed_out, quarter)


def once(shape):
    n = len(shape)
    return pl.BlockSpec(shape, lambda i: (0,) * n, pipeline_mode=pl.Buffered(buffer_count=1))


def expert_call(packed, weight_in, weight_out):
    width, both = weight_in.shape
    hidden = both // 2
    steps = 2
    block = packed.shape[0] // steps
    real = block * SLOTS // GROUP
    part = packed.shape[1] // 2
    at = lambda i: (i, 0)
    return call(
        expert_body,
        "expert",
        (
            sds((real * steps, width), BF),
            sds((real * steps, width), BF),
            sds((real * steps, hidden), BF),
            sds((real * steps, both), BF),
            sds((packed.shape[0], part), BF),
        ),
        (steps,),
        [
            pl.BlockSpec((block, part), at),
            pl.BlockSpec((block, part), lambda i: (i, 1)),
            once(weight_in.shape),
            once(weight_out.shape),
        ],
        (
            pl.BlockSpec((real, width), at),
            pl.BlockSpec((real, width), at),
            pl.BlockSpec((real, hidden), at),
            pl.BlockSpec((real, both), at),
            pl.BlockSpec((block, part), at),
        ),
        flops=5 * real * steps * both * width,
        nbytes=2 * both * width + 10 * real * steps * width,
    )(packed, packed, weight_in, weight_out)


def expert_y_body(act, weight_out, packed_out):
    rows = mm(act[...], weight_out[...]).astype(BF)
    repack_rows(rows, packed_out, weight_out.shape[1] // 4)


def expert_y_call(act, weight_out):
    hidden, width = weight_out.shape
    steps = 2
    real = act.shape[0] // steps
    block = real * GROUP // SLOTS
    at = lambda i: (i, 0)
    return call(
        expert_y_body,
        "expert_y",
        sds((block * steps, width * 3 // 4), BF),
        (steps,),
        [pl.BlockSpec((real, hidden), at), whole(weight_out.shape)],
        pl.BlockSpec((block, width * 3 // 4), at),
        flops=2 * real * steps * hidden * width,
        nbytes=2 * hidden * width + 4 * real * steps * width,
    )(act, weight_out)


def rows_of(ref, order, places):
    return jnp.concatenate([ref[order[p]] for p in places], axis=0)


def product(order, places, ctx_own, ctx_got, w_own, w_got, cols):
    own = mm(rows_of(ctx_own, order, places), w_own[:, cols])
    return own + mm(rows_of(ctx_got, order, places), w_got[:, cols])


def halves(w):
    half = w.shape[1] // 2
    return slice(0, half), slice(half, 2 * half)


def project_first_body(order, ctx_own, ctx_got, w_own, w_got, over_z, *over_x):
    left, right = halves(w_own)
    args = (ctx_own, ctx_got, w_own, w_got)
    over_z[...] = product(order, [1, 3, 5, 7], *args, left).astype(BF)
    for d in range(3):
        over_x[d][...] = product(order, [2 * d + 2, 2 * d + 3], *args, right).astype(BF)


def project_keep_body(order, ctx_own, ctx_got, w_own, w_got, keep_a, keep_b):
    left, right = halves(w_own)
    args = (ctx_own, ctx_got, w_own, w_got)
    keep_b[...] = product(order, [0, 1], *args, right)
    keep_a[...] = product(order, [0, 2, 4, 6], *args, left)


def add_body(order, kept_a, kept_b, got_z, got_1, got_2, got_3, keep_a, keep_b, over_z, *over_x):
    tok = keep_a.shape[0]
    keep_a[...] = kept_a[0:tok, :] + got_z[0:tok, :].astype(F32)
    for d in range(3):
        at = slice((d + 1) * tok, (d + 2) * tok)
        over_x[d][...] = (kept_a[at, :] + got_z[at, :].astype(F32)).astype(BF)
    total = kept_b[...]
    for got in (got_1, got_2, got_3):
        total = total + got[...].astype(F32)
    keep_b[...] = total[:tok]
    over_z[...] = total[tok:].astype(BF)


def plain(body, name, outs, order, *args, flops=0, scratch=()):
    nbytes = sum(a.size * a.dtype.itemsize for a in args)
    nbytes += sum(o.size * o.dtype.itemsize for o in outs)
    return call(
        body,
        name,
        tuple(outs),
        (1,),
        [pl.BlockSpec(memory_space=pltpu.SMEM)] + [whole(a.shape) for a in args],
        tuple(whole(o.shape) for o in outs),
        scratch,
        flops=flops,
        nbytes=nbytes,
    )(order, *args)


N_BLOCKS = 11


def gather_parts(blocks, first, last):
    same_z, other_z, left_z, right_z = blocks[:4], blocks[4], blocks[5:8], blocks[8:]
    cut = left_z[0].shape[1]
    left, right = [], []
    for d in range(4):
        left += [same_z[d][first:last, :cut]]
        left += [left_z[d - 1][first:last, :] if d else other_z[first:last, :cut]]
        right += [same_z[d][first:last, cut:]]
        right += [right_z[d - 1][first:last, :] if d else other_z[first:last, cut:]]
    return left, right


def gather_rows(blocks):
    left, right = gather_parts(blocks, 0, blocks[0].shape[0] - 16)
    return jnp.concatenate(left, axis=0), jnp.concatenate(right, axis=0)


def weight_give_body(order, ctx_got, *refs):
    blocks, (give, gain_out) = refs[:N_BLOCKS], refs[N_BLOCKS:]
    tok = ctx_got.shape[1]
    ctx = rows_of(ctx_got, order, range(8))
    gains = gather_parts(blocks, tok, tok + 16)
    first = 0
    for h, rows in enumerate(gather_rows(blocks)):
        last = first + rows.shape[1]
        give[:, first:last] = mm(ctx, rows, 0, 0).astype(BF)
        total = jnp.zeros((16, last - first), F32)
        for part in gains[h]:
            total = total + part.astype(F32)
        total = jnp.sum(total, axis=0, keepdims=True)
        gain_out[:, first:last] = jnp.broadcast_to(total, (8, last - first))
        first = last


def context_grad_body(order, w_own, w_got, *refs):
    blocks, (own, give) = refs[:N_BLOCKS], refs[N_BLOCKS:]
    tok = own.shape[1]
    left, right = gather_rows(blocks)
    cut = left.shape[1]
    for w, out in ((w_got, give), (w_own, own)):
        grad = mm(left, w[:, :cut], 1, 1) + mm(right, w[:, cut:], 1, 1)
        grad = grad.astype(BF)
        for p in range(8):
            out[order[p] // 2] = grad[p * tok : (p + 1) * tok]


def weight_own_body(order, ctx_own, got, gain_own, gain_got, *refs):
    blocks, outs, held = refs[:N_BLOCKS], refs[N_BLOCKS:-1], refs[-1]
    cols = ctx_own.shape[2]
    n_ctx, _, width = held.shape
    ctx = rows_of(ctx_own, order, range(8))
    parts = thirds(gain_own[0:1, :] + gain_got[0:1, :])
    row = iota((32, width), 0)
    gain = jnp.zeros((32, width), F32)
    for p in range(3):
        for j in range(n_ctx):
            piece = parts[p][:, j * width : (j + 1) * width].astype(F32)
            gain = jnp.where(row == p * n_ctx + j, piece, gain)
    gain = gain.astype(BF)
    first = 0
    for rows in gather_rows(blocks):
        last = first + rows.shape[1]
        grad = mm(ctx, rows, 0, 0) + got[:, first:last].astype(F32)
        grad = grad.astype(BF)
        for j in range(first // width, last // width):
            held[j, 0:cols, :] = grad[:, j * width - first : (j + 1) * width - first]
            held[j, cols : cols + 32, :] = gain
        first = last
    y, z = order[8] // 2, order[8] % 2
    for d, out in enumerate(outs):
        for o in range(2):
            out[o] = held[(y + d) % (n_ctx // 2) * 2 + (z + o) % 2]


def trade(values):
    n_all = lax.axis_size("ctx") * lax.axis_size("tp")
    shaped = values.reshape(n_all, GROUP, values.shape[1])
    moved = lax.all_to_all(shaped, ("ctx", "tp"), split_axis=0, concat_axis=0, tiled=True)
    return moved.reshape(values.shape)


def on_device(
    context, residual, o_weight, norm_gain, routes, gate_weights, expert_in, expert_out, cotangent
):
    tok, width = residual.shape
    n_tp = lax.axis_size("tp")
    n_ctx = lax.axis_size("ctx")
    n_exp = n_tp * n_ctx
    chips = n_tp // 2
    cols = context.shape[1]
    core = lax.axis_index("tp") % 2
    gain_row = norm_gain.reshape(1, width)

    t = lax.axis_index("tp")
    x, z = t // 4, t // 2 % 2
    pairs = [(d, o) for d in range(4) for o in range(2)]
    order = jnp.stack([(x + d) % 4 * 4 + (z ^ o) * 2 + core for d, o in pairs])
    came = jnp.stack([(x - d) % 4 * 4 + (z ^ o) * 2 + core for d, o in pairs])

    def over_x(d):
        return [(u, (u + 4 * d) % n_tp) for u in range(n_tp)]

    over_z = [(u, u ^ 2) for u in range(n_tp)]
    swap = [(u, u ^ 1) for u in range(n_tp)]

    def move(values, perm):
        return lax.ppermute(values, "tp", perm)

    ctx_own = context.reshape(n_tp, tok, cols)
    ctx_got = move(ctx_own, swap)
    w_got = move(o_weight, swap)
    packed_g = pack_grads(routes, gate_weights, cotangent, n_exp)
    half = width // 2
    operands = (ctx_own, ctx_got, o_weight, w_got)
    per_block = 4 * tok * cols * half
    send_z, *send_x = plain(
        project_first_body,
        "project_first",
        [sds((4 * tok, half), BF)] + [sds((2 * tok, half), BF)] * 3,
        order,
        *operands,
        flops=10 * per_block,
    )
    got_z = move(send_z, over_z)
    got_x = [move(send_x[d], over_x(d + 1)) for d in range(3)]
    kept_a, kept_b = plain(
        project_keep_body,
        "project_keep",
        [sds((4 * tok, half), F32), sds((2 * tok, half), F32)],
        order,
        *operands,
        flops=6 * per_block,
    )
    keep_a, keep_b, send_b, *send_a = plain(
        add_body,
        "add",
        [sds((tok, half), F32)] * 2 + [sds((tok, half), BF)] * 4,
        order,
        kept_a,
        kept_b,
        got_z,
        *got_x,
    )
    got_a = [move(send_a[d], over_x(d + 1)) for d in range(3)]
    got_b = move(send_b, over_z)

    packed_h, mixed = norm_pack(
        routes, keep_a, keep_b, got_a, got_b, residual, gain_row, packed_g, n_exp
    )
    rows_in = trade(packed_h)

    weight_in, weight_out = expert_in[0], expert_out[0]
    arrived, grads, act, ggu, packed_back = expert_call(rows_in, weight_in, weight_out)
    back = trade(packed_back)
    packed_y = expert_y_call(act, weight_out)
    d_expert_out = contract(act, grads, 0, 0).astype(BF)[None]
    d_expert_in = contract(arrived, ggu, 0, 0).astype(BF)[None]
    back, packed_y, d_expert_out, d_expert_in = lax.optimization_barrier(
        (back, packed_y, d_expert_out, d_expert_in)
    )
    res, d_residual = combine_grads(routes, back, mixed, gain_row, cotangent, n_exp)

    same_z = [res] + [move(res, over_x(d)) for d in range(1, 4)]
    other_z = move(res, over_z)
    cut = width * 3 // 8
    left_z = [move(v[:, :cut], over_z) for v in same_z[1:]]
    right_z = [move(other_z[:, cut:], over_x(d)) for d in range(1, 4)]
    blocks = [*same_z, other_z, *left_z, *right_z]
    packed_y, *blocks = lax.optimization_barrier((packed_y, *blocks))
    y_back = trade(packed_y)

    w_give, gain_own = plain(
        weight_give_body,
        "weight_give",
        [sds((cols, width), BF), sds((8, width), F32)],
        came,
        ctx_got,
        *blocks,
        flops=16 * tok * cols * width,
    )
    w_grad_got = move(w_give, swap)
    gain_got = move(gain_own, swap)
    out_cols = width // n_ctx
    part = (cols + 32, out_cols)
    sent = plain(
        weight_own_body,
        "weight_own",
        [sds((2,) + part, BF)] * (n_ctx // 2),
        jnp.concatenate([came, lax.axis_index("ctx").reshape(1)]),
        ctx_own,
        w_grad_got,
        gain_own,
        gain_got,
        *blocks,
        flops=16 * tok * cols * width,
        scratch=[pltpu.VMEM((n_ctx,) + part, BF)],
    )
    ctx_mine, ctx_grad_give = plain(
        context_grad_body,
        "context_grad",
        [sds((chips, tok, cols), BF)] * 2,
        came,
        o_weight,
        w_got,
        *blocks,
        flops=32 * tok * cols * width,
    )
    ctx_other = move(ctx_grad_give, swap)
    over_y = [sent[0]]
    for d in range(1, n_ctx // 2):
        around = [(u, (u + 2 * d) % n_ctx) for u in range(n_ctx)]
        over_y.append(lax.ppermute(sent[d], "ctx", around))
    layer_out = combine_out(routes, gate_weights, y_back, mixed, n_exp)
    summed = sum(f.astype(F32) for f in over_y)
    other = summed[1].astype(BF)
    last = lax.ppermute(other, "ctx", [(u, u ^ 1) for u in range(n_ctx)])
    layer_out, last = lax.optimization_barrier((layer_out, last))
    final = summed[0] + last.astype(F32)
    d_o_weight = final[:cols]
    d_gain = jnp.sum(final[cols : cols + 3 * n_ctx].reshape(3, width), axis=0)

    mine = ctx_mine.reshape(chips, 1, tok, cols)
    other = ctx_other.reshape(chips, 1, tok, cols)
    d_context = jnp.where(
        core == 0,
        jnp.concatenate([mine, other], axis=1),
        jnp.concatenate([other, mine], axis=1),
    ).reshape(context.shape)
    return (layer_out, d_context, d_residual, d_o_weight, d_gain, d_expert_in, d_expert_out)


def solution(mesh):
    rows = P(("ctx", "tp"), None)
    experts = P(("ctx", "tp"), None, None)
    in_specs = (P("ctx", "tp"), rows, P("tp", None), P(), rows, rows, experts, experts, rows)
    out_specs = (rows, P("ctx", "tp"), rows, P("tp", "ctx"), P(), experts, experts)
    return jax.shard_map(
        on_device, mesh=mesh, in_specs=in_specs, out_specs=out_specs, check_vma=False
    )
```

```python
import functools

import jax
import jax.numpy as jnp
from jax import lax
from jax.experimental import pallas as pl
from jax.experimental.pallas import tpu as pltpu
from jax.sharding import PartitionSpec as P

BF = jnp.bfloat16
F32 = jnp.float32
SLOTS = 6
GROUP = 8
PACK = 3
MIB = 1024 * 1024
LANES = 128
BIG = ("expert", "expert_y", "weight_give", "weight_own", "context_grad")


def mm(a, b, da=1, db=0):
    return lax.dot_general(a, b, (((da,), (db,)), ((), ())), preferred_element_type=F32)


def contract(left_arr, right_arr, left_dim, right_dim):
    return mm(left_arr, right_arr, left_dim, right_dim)


def iota(shape, dim):
    return lax.broadcasted_iota(jnp.int32, shape, dim)


def call(body, name, out, grid, in_specs, out_specs, scratch=(), flops=0, nbytes=0):
    return pl.pallas_call(
        body,
        out_shape=out,
        grid_spec=pltpu.PrefetchScalarGridSpec(
            num_scalar_prefetch=0,
            grid=grid,
            in_specs=in_specs,
            out_specs=out_specs,
            scratch_shapes=scratch,
        ),
        compiler_params=pltpu.CompilerParams(
            dimension_semantics=("arbitrary",) * len(grid), vmem_limit_bytes=(56 if name in BIG else 26) * MIB
        ),
        cost_estimate=pl.CostEstimate(flops=flops, bytes_accessed=nbytes, transcendentals=0),
        name=name,
    )


def whole(shape):
    n = len(shape)
    return pl.BlockSpec(shape, lambda i: (0,) * n)


def sds(shape, dtype):
    return jax.ShapeDtypeStruct(shape, dtype)


def slot_table(routes, n_exp):
    rows = routes.shape[0]
    lane = iota((rows, n_exp), 1)
    named = jnp.zeros((rows, n_exp), F32)
    for k in range(routes.shape[1]):
        named = named + (routes[:, k : k + 1] == lane).astype(F32)
    before = (iota((rows, rows), 0) > iota((rows, rows), 1)).astype(BF)
    rank = mm(before, named.astype(BF))
    return jnp.where(named > 0, rank, -1.0)


def gate_table(routes, gates, n_exp):
    rows = routes.shape[0]
    lane = iota((rows, n_exp), 1)
    table = jnp.zeros((rows, n_exp), F32)
    for k in range(routes.shape[1]):
        table = table + jnp.where(routes[:, k : k + 1] == lane, gates[:, k : k + 1], 0.0)
    return table


def thirds(values):
    high = values.astype(BF)
    rest = values - high.astype(F32)
    middle = rest.astype(BF)
    low = (rest - middle.astype(F32)).astype(BF)
    return high, middle, low


def pick_rows(slot, first, count):
    rows, n_exp = slot.shape
    row = iota((count, n_exp), 0) + first
    spread = (row // GROUP == iota((count, n_exp), 1)).astype(BF)
    at = mm(spread, slot.astype(BF), 1, 1)
    place = (iota((count, rows), 0) % GROUP).astype(F32)
    main = (at == place) & (place < SLOTS)
    tails = [(at == (place - SLOTS) * PACK + c) & (place >= SLOTS) for c in range(PACK)]
    return spread, main, tails


def pack_tokens(values, main, tails, quarter):
    out = []
    last = values[:, PACK * quarter :]
    for c in range(PACK):
        pick = jnp.concatenate([main.astype(BF), tails[c].astype(BF)], axis=1)
        source = jnp.concatenate([values[:, c * quarter : (c + 1) * quarter], last], axis=0)
        out.append(mm(pick, source))
    return out


def block_perm(count):
    real = count * SLOTS // GROUP
    row, col = iota((real, count), 0), iota((real, count), 1)
    owner, slot = row // SLOTS, row % SLOTS
    same = owner == col // GROUP
    place = col % GROUP
    main = same & (place == slot)
    tails = [
        same & (place == SLOTS + slot // PACK) & (slot % PACK == c) for c in range(PACK)
    ]
    return main.astype(BF), [t.astype(BF) for t in tails]


def block_perm_back(count):
    real = count * SLOTS // GROUP
    row, col = iota((count, real), 0), iota((count, real), 1)
    place, slot = row % GROUP, col % SLOTS
    same = row // GROUP == col // SLOTS
    main = same & (place == slot)
    tails = [
        same & (place == SLOTS + slot // PACK) & (slot % PACK == c) for c in range(PACK)
    ]
    return [jnp.concatenate([main.astype(BF), t.astype(BF)], axis=1) for t in tails]


def unpack(packed, perm, quarter):
    main, tails = perm
    head = mm(main, packed).astype(BF)
    stack = jnp.concatenate([packed[:, c * quarter : (c + 1) * quarter] for c in range(PACK)], axis=0)
    tail = mm(jnp.concatenate(tails, axis=1), stack).astype(BF)
    return jnp.concatenate([head, tail], axis=1)


def repack(rows, perm, quarter):
    last = rows[:, PACK * quarter :]
    out = []
    for c in range(PACK):
        source = jnp.concatenate([rows[:, c * quarter : (c + 1) * quarter], last], axis=0)
        out.append(mm(perm[c], source).astype(BF))
    return jnp.concatenate(out, axis=1)


def pack_grads_body(n_exp, rows, routes, gates, cot, out, slot, high, middle, low):
    i = pl.program_id(0)

    @pl.when(i == 0)
    def _():
        slot[...] = slot_table(routes[...], n_exp)
        high[...], middle[...], low[...] = thirds(gate_table(routes[...], gates[...], n_exp))

    quarter = cot.shape[1] // 4
    spread, main, tails = pick_rows(slot[...], i * rows, rows)
    gate = (mm(spread, high[...], 1, 1) + mm(spread, middle[...], 1, 1)) + mm(spread, low[...], 1, 1)
    parts = pack_tokens(cot[...], main, tails, quarter)
    for c in range(PACK):
        own = jnp.sum(jnp.where(main | tails[c], gate, 0.0), axis=1, keepdims=True)
        out[:, c * quarter : (c + 1) * quarter] = (parts[c] * own).astype(BF)


def pack_grads(routes, gates, cot, n_exp):
    tok, width = cot.shape
    total, steps = n_exp * GROUP, 4
    rows = total // steps
    table = pltpu.VMEM((tok, n_exp), BF)
    return call(
        functools.partial(pack_grads_body, n_exp, rows),
        "pack_grads",
        sds((total, width * 3 // 4), BF),
        (steps,),
        [whole(routes.shape), whole(gates.shape), whole(cot.shape)],
        pl.BlockSpec((rows, width * 3 // 4), lambda i: (i, 0)),
        [pltpu.VMEM((tok, n_exp), F32), table, table, table],
        flops=2 * total * 2 * tok * width,
        nbytes=8 * total * width,
    )(routes, gates, cot)


def norm_pack_body(n_exp, rows, routes, keep_a, keep_b, *refs):
    got_a, got_b, residual, gain, packed_g, out, mixed_out, slot, normed_h = (
        refs[:3], refs[3], *refs[4:]
    )
    i = pl.program_id(0)

    @pl.when(i == 0)
    def _():
        slot[...] = slot_table(routes[...], n_exp)
        tok, width = residual.shape
        step = 32

        def norm(j, carry):
            at = pl.ds(pl.multiple_of(j * step, step), step)
            left = keep_a[at, :]
            for part in got_a:
                left = left + part[at, :].astype(F32)
            right = keep_b[at, :] + got_b[at, :].astype(F32)
            total = jnp.concatenate([left, right], axis=1)
            mixed = (residual[at, :].astype(F32) + total).astype(BF)
            mixed_out[at, :] = mixed
            mixed = mixed.astype(F32)
            inv_rms = lax.rsqrt(jnp.mean(mixed * mixed, axis=-1, keepdims=True) + 1e-06)
            normed_h[at, :] = (mixed * inv_rms * gain[...].astype(F32)).astype(BF)
            return carry

        lax.fori_loop(0, tok // step, norm, 0)

    quarter = residual.shape[1] // 4
    _, main, tails = pick_rows(slot[...], i * rows, rows)
    packed = pack_tokens(normed_h[...], main, tails, quarter)
    for c in range(PACK):
        out[:, c * quarter : (c + 1) * quarter] = packed[c].astype(BF)
    out[:, PACK * quarter :] = packed_g[...]


def norm_pack(routes, keep_a, keep_b, got_a, got_b, residual, gain, packed_g, n_exp):
    tok, width = residual.shape
    total, steps = n_exp * GROUP, 4
    rows = total // steps
    args = (routes, keep_a, keep_b, *got_a, got_b, residual, gain)
    return call(
        functools.partial(norm_pack_body, n_exp, rows),
        "norm_pack",
        (sds((total, width * 3 // 2), BF), sds((tok, width), BF)),
        (steps,),
        [whole(a.shape) for a in args] + [pl.BlockSpec((rows, width * 3 // 4), lambda i: (i, 0))],
        (pl.BlockSpec((rows, width * 3 // 2), lambda i: (i, 0)), whole((tok, width))),
        [pltpu.VMEM((tok, n_exp), F32), pltpu.VMEM((tok, width), BF)],
        flops=2 * total * 2 * tok * width,
        nbytes=8 * total * width,
    )(*args, packed_g)


def pick_tokens(slot):
    rows, n_exp = slot.shape
    total = n_exp * GROUP
    spread = (iota((n_exp, total), 1) // GROUP == iota((n_exp, total), 0)).astype(BF)
    at = mm(slot.astype(BF), spread)
    place = (iota((rows, total), 1) % GROUP).astype(F32)
    main = (at == place) & (place < SLOTS)
    tails = [(at == (place - SLOTS) * PACK + c) & (place >= SLOTS) for c in range(PACK)]
    return spread, main, tails


def combine_grads_body(n_exp, routes, packed, mixed_ref, gain, cot, out, res_out):
    tok, width = cot.shape
    quarter = width // 4
    _, main, tails = pick_tokens(slot_table(routes[...], n_exp))
    heads, last = [], jnp.zeros((tok, quarter), F32)
    for c in range(PACK):
        pick = jnp.concatenate([main.astype(BF), tails[c].astype(BF)], axis=0)
        both = mm(pick, packed[:, c * quarter : (c + 1) * quarter])
        heads.append(both[:tok])
        last = last + both[tok:]
    grad_h = jnp.concatenate(heads + [last], axis=1)
    mixed = mixed_ref[...].astype(F32)
    inv_rms = lax.rsqrt(jnp.mean(mixed * mixed, axis=-1, keepdims=True) + 1e-06)
    normed = mixed * inv_rms
    d_gain = jnp.sum(grad_h * normed, axis=0, keepdims=True)
    gain_cols = jnp.zeros((tok, LANES), F32)
    row = iota((tok, LANES), 0)
    per = width // LANES
    for p, part in enumerate(thirds(d_gain)):
        for q in range(per):
            piece = part[:, q * LANES : (q + 1) * LANES].astype(F32)
            gain_cols = jnp.where(row == p * per + q, piece, gain_cols)
    grad_n = grad_h * gain[...].astype(F32)
    inner = jnp.mean(grad_n * normed, axis=-1, keepdims=True)
    d_res = cot[...].astype(F32) + inv_rms * (grad_n - normed * inner)
    d_res = d_res.astype(BF)
    res_out[...] = d_res
    out[:, :width] = d_res
    out[:, width:] = gain_cols.astype(BF)


def combine_grads(routes, packed, mixed, gain, cot, n_exp):
    tok, width = cot.shape
    return call(
        functools.partial(combine_grads_body, n_exp),
        "combine_grads",
        (sds((tok, width + LANES), BF), sds((tok, width), BF)),
        (1,),
        [whole(a.shape) for a in (routes, packed, mixed, gain, cot)],
        (whole((tok, width + LANES)), whole((tok, width))),
        flops=2 * packed.shape[0] * 2 * tok * width,
        nbytes=8 * packed.shape[0] * width,
    )(routes, packed, mixed, gain, cot)


def combine_out_body(n_exp, routes, gates, packed, mixed, out):
    tok, width = mixed.shape
    quarter = width // 4
    spread, main, tails = pick_tokens(slot_table(routes[...], n_exp))
    parts = thirds(gate_table(routes[...], gates[...], n_exp))
    gate = (mm(parts[0], spread) + mm(parts[1], spread)) + mm(parts[2], spread)
    high = gate.astype(BF)
    low = (gate - high.astype(F32)).astype(BF)
    none = jnp.zeros_like(high)
    last = jnp.zeros((tok, quarter), F32)
    for c in range(PACK):
        pick = jnp.concatenate(
            [
                jnp.where(main, high, none),
                jnp.where(main, low, none),
                jnp.where(tails[c], high, none),
                jnp.where(tails[c], low, none),
            ],
            axis=0,
        )
        both = mm(pick, packed[:, c * quarter : (c + 1) * quarter])
        at = slice(c * quarter, (c + 1) * quarter)
        head = both[:tok] + both[tok : 2 * tok]
        out[:, at] = (mixed[:, at].astype(F32) + head).astype(BF)
        last = last + (both[2 * tok : 3 * tok] + both[3 * tok :])
    at = slice(PACK * quarter, width)
    out[:, at] = (mixed[:, at].astype(F32) + last).astype(BF)


def combine_out(routes, gates, packed, mixed, n_exp):
    tok, width = mixed.shape
    return call(
        functools.partial(combine_out_body, n_exp),
        "combine_out",
        sds((tok, width), BF),
        (1,),
        [whole(a.shape) for a in (routes, gates, packed, mixed)],
        whole((tok, width)),
        flops=2 * packed.shape[0] * 4 * tok * width,
        nbytes=6 * packed.shape[0] * width,
    )(routes, gates, packed, mixed)


SUB = 256


def unpack_rows(packed, quarter):
    perm = block_perm(SUB)
    return jnp.concatenate(
        [
            unpack(packed[j * SUB : (j + 1) * SUB, :], perm, quarter)
            for j in range(packed.shape[0] // SUB)
        ],
        axis=0,
    )


def repack_rows(rows, out, quarter):
    perm = block_perm_back(SUB)
    real = SUB * SLOTS // GROUP
    for j in range(rows.shape[0] // real):
        out[j * SUB : (j + 1) * SUB, :] = repack(rows[j * real : (j + 1) * real, :], perm, quarter)


def expert_body(
    packed_h, packed_g, weight_in, weight_out, rows_out, grads_out, act_out, ggu_out, packed_out
):
    width, both = weight_in.shape
    hidden = both // 2
    quarter = width // 4
    rows = unpack_rows(packed_h, quarter)
    rows_out[...] = rows
    gate_part = mm(rows, weight_in[:, :hidden])
    up_part = mm(rows, weight_in[:, hidden:])
    sigma = jax.nn.sigmoid(gate_part)
    silu = gate_part * sigma
    act_out[...] = (silu * up_part).astype(BF)
    grads = unpack_rows(packed_g, quarter)
    grads_out[...] = grads
    grad_act = mm(grads, weight_out[...], 1, 1)
    grad_gate = (grad_act * up_part * sigma * (1.0 + gate_part * (1.0 - sigma))).astype(BF)
    grad_up = (grad_act * silu).astype(BF)
    ggu_out[:, :hidden] = grad_gate
    ggu_out[:, hidden:] = grad_up
    back = mm(jnp.concatenate([grad_gate, grad_up], axis=1), weight_in[...], 1, 1).astype(BF)
    repack_rows(back, packed_out, quarter)


def once(shape):
    n = len(shape)
    return pl.BlockSpec(shape, lambda i: (0,) * n, pipeline_mode=pl.Buffered(buffer_count=1))


def expert_call(packed, weight_in, weight_out):
    width, both = weight_in.shape
    hidden = both // 2
    steps = 2
    block = packed.shape[0] // steps
    real = block * SLOTS // GROUP
    part = packed.shape[1] // 2
    at = lambda i: (i, 0)
    return call(
        expert_body,
        "expert",
        (
            sds((real * steps, width), BF),
            sds((real * steps, width), BF),
            sds((real * steps, hidden), BF),
            sds((real * steps, both), BF),
            sds((packed.shape[0], part), BF),
        ),
        (steps,),
        [
            pl.BlockSpec((block, part), at),
            pl.BlockSpec((block, part), lambda i: (i, 1)),
            once(weight_in.shape),
            once(weight_out.shape),
        ],
        (
            pl.BlockSpec((real, width), at),
            pl.BlockSpec((real, width), at),
            pl.BlockSpec((real, hidden), at),
            pl.BlockSpec((real, both), at),
            pl.BlockSpec((block, part), at),
        ),
        flops=5 * real * steps * both * width,
        nbytes=2 * both * width + 10 * real * steps * width,
    )(packed, packed, weight_in, weight_out)


def expert_y_body(act, weight_out, packed_out):
    rows = mm(act[...], weight_out[...]).astype(BF)
    repack_rows(rows, packed_out, weight_out.shape[1] // 4)


def expert_y_call(act, weight_out):
    hidden, width = weight_out.shape
    steps = 2
    real = act.shape[0] // steps
    block = real * GROUP // SLOTS
    at = lambda i: (i, 0)
    return call(
        expert_y_body,
        "expert_y",
        sds((block * steps, width * 3 // 4), BF),
        (steps,),
        [pl.BlockSpec((real, hidden), at), whole(weight_out.shape)],
        pl.BlockSpec((block, width * 3 // 4), at),
        flops=2 * real * steps * hidden * width,
        nbytes=2 * hidden * width + 4 * real * steps * width,
    )(act, weight_out)


def rows_of(ref, order, places):
    return jnp.concatenate([ref[order[p]] for p in places], axis=0)


def product(order, places, ctx_own, ctx_got, w_own, w_got, cols):
    own = mm(rows_of(ctx_own, order, places), w_own[:, cols])
    return own + mm(rows_of(ctx_got, order, places), w_got[:, cols])


def halves(w):
    half = w.shape[1] // 2
    return slice(0, half), slice(half, 2 * half)


def project_first_body(order, ctx_own, ctx_got, w_own, w_got, over_z, *over_x):
    left, right = halves(w_own)
    args = (ctx_own, ctx_got, w_own, w_got)
    over_z[...] = product(order, [1, 3, 5, 7], *args, left).astype(BF)
    for d in range(3):
        over_x[d][...] = product(order, [2 * d + 2, 2 * d + 3], *args, right).astype(BF)


def project_keep_body(order, ctx_own, ctx_got, w_own, w_got, keep_a, keep_b):
    left, right = halves(w_own)
    args = (ctx_own, ctx_got, w_own, w_got)
    keep_b[...] = product(order, [0, 1], *args, right)
    keep_a[...] = product(order, [0, 2, 4, 6], *args, left)


def add_body(order, kept_a, kept_b, got_z, got_1, got_2, got_3, keep_a, keep_b, over_z, *over_x):
    tok = keep_a.shape[0]
    keep_a[...] = kept_a[0:tok, :] + got_z[0:tok, :].astype(F32)
    for d in range(3):
        at = slice((d + 1) * tok, (d + 2) * tok)
        over_x[d][...] = (kept_a[at, :] + got_z[at, :].astype(F32)).astype(BF)
    total = kept_b[...]
    for got in (got_1, got_2, got_3):
        total = total + got[...].astype(F32)
    keep_b[...] = total[:tok]
    over_z[...] = total[tok:].astype(BF)


def plain(body, name, outs, order, *args, flops=0, scratch=()):
    nbytes = sum(a.size * a.dtype.itemsize for a in args)
    nbytes += sum(o.size * o.dtype.itemsize for o in outs)
    return call(
        body,
        name,
        tuple(outs),
        (1,),
        [pl.BlockSpec(memory_space=pltpu.SMEM)] + [whole(a.shape) for a in args],
        tuple(whole(o.shape) for o in outs),
        scratch,
        flops=flops,
        nbytes=nbytes,
    )(order, *args)


N_BLOCKS = 11


def gather_rows(blocks):
    same_z, other_z, left_z, right_z = blocks[:4], blocks[4], blocks[5:8], blocks[8:]
    width, cut = other_z.shape[1] - LANES, left_z[0].shape[1]
    left, right = [], []
    for d in range(4):
        left += [same_z[d][:, :cut], left_z[d - 1][...] if d else other_z[:, :cut]]
        right += [same_z[d][:, cut:width]]
        right += [right_z[d - 1][:, : width - cut] if d else other_z[:, cut:width]]
    return jnp.concatenate(left, axis=0), jnp.concatenate(right, axis=0)


def gather_gain(blocks):
    total = jnp.zeros((blocks[0].shape[0], LANES), F32)
    for block in blocks[:5] + blocks[8:]:
        total = total + block[:, block.shape[1] - LANES :].astype(F32)
    per = (blocks[0].shape[1] - LANES) // LANES
    rows = []
    for q in range(per):
        high, middle, low = [total[p * per + q : p * per + q + 1, :] for p in range(3)]
        rows.append(high + middle + low)
    return jnp.concatenate(rows, axis=1)


def weight_give_body(order, ctx_got, *refs):
    blocks, (give, gain_out) = refs[:N_BLOCKS], refs[N_BLOCKS:]
    ctx = rows_of(ctx_got, order, range(8))
    first = 0
    for rows in gather_rows(blocks):
        last = first + rows.shape[1]
        give[:, first:last] = mm(ctx, rows, 0, 0).astype(BF)
        first = last
    gain_out[...] = jnp.broadcast_to(gather_gain(blocks), gain_out.shape)


def context_grad_body(order, w_own, w_got, *refs):
    blocks, (own, give) = refs[:N_BLOCKS], refs[N_BLOCKS:]
    tok = own.shape[1]
    left, right = gather_rows(blocks)
    cut = left.shape[1]
    for w, out in ((w_got, give), (w_own, own)):
        grad = mm(left, w[:, :cut], 1, 1) + mm(right, w[:, cut:], 1, 1)
        grad = grad.astype(BF)
        for p in range(8):
            out[order[p] // 2] = grad[p * tok : (p + 1) * tok]


def weight_own_body(order, ctx_own, got, gain_own, gain_got, *refs):
    blocks, outs, held = refs[:N_BLOCKS], refs[N_BLOCKS:-1], refs[-1]
    cols = ctx_own.shape[2]
    n_ctx, _, width = held.shape
    ctx = rows_of(ctx_own, order, range(8))
    parts = thirds(gain_own[0:1, :] + gain_got[0:1, :])
    row = iota((32, width), 0)
    gain = jnp.zeros((32, width), F32)
    for p in range(3):
        for j in range(n_ctx):
            piece = parts[p][:, j * width : (j + 1) * width].astype(F32)
            gain = jnp.where(row == p * n_ctx + j, piece, gain)
    gain = gain.astype(BF)
    first = 0
    for rows in gather_rows(blocks):
        last = first + rows.shape[1]
        grad = mm(ctx, rows, 0, 0) + got[:, first:last].astype(F32)
        grad = grad.astype(BF)
        for j in range(first // width, last // width):
            held[j, 0:cols, :] = grad[:, j * width - first : (j + 1) * width - first]
            held[j, cols : cols + 32, :] = gain
        first = last
    y, z = order[8] // 2, order[8] % 2
    for d, out in enumerate(outs):
        for o in range(2):
            out[o] = held[(y + d) % (n_ctx // 2) * 2 + (z + o) % 2]


def trade(values):
    n_all = lax.axis_size("ctx") * lax.axis_size("tp")
    shaped = values.reshape(n_all, GROUP, values.shape[1])
    moved = lax.all_to_all(shaped, ("ctx", "tp"), split_axis=0, concat_axis=0, tiled=True)
    return moved.reshape(values.shape)


def on_device(
    context, residual, o_weight, norm_gain, routes, gate_weights, expert_in, expert_out, cotangent
):
    tok, width = residual.shape
    n_tp = lax.axis_size("tp")
    n_ctx = lax.axis_size("ctx")
    n_exp = n_tp * n_ctx
    chips = n_tp // 2
    cols = context.shape[1]
    core = lax.axis_index("tp") % 2
    gain_row = norm_gain.reshape(1, width)

    t = lax.axis_index("tp")
    x, z = t // 4, t // 2 % 2
    pairs = [(d, o) for d in range(4) for o in range(2)]
    order = jnp.stack([(x + d) % 4 * 4 + (z ^ o) * 2 + core for d, o in pairs])
    came = jnp.stack([(x - d) % 4 * 4 + (z ^ o) * 2 + core for d, o in pairs])

    def over_x(d):
        return [(u, (u + 4 * d) % n_tp) for u in range(n_tp)]

    over_z = [(u, u ^ 2) for u in range(n_tp)]
    swap = [(u, u ^ 1) for u in range(n_tp)]

    def move(values, perm):
        return lax.ppermute(values, "tp", perm)

    ctx_own = context.reshape(n_tp, tok, cols)
    ctx_got = move(ctx_own, swap)
    w_got = move(o_weight, swap)
    packed_g = pack_grads(routes, gate_weights, cotangent, n_exp)
    half = width // 2
    operands = (ctx_own, ctx_got, o_weight, w_got)
    per_block = 4 * tok * cols * half
    send_z, *send_x = plain(
        project_first_body,
        "project_first",
        [sds((4 * tok, half), BF)] + [sds((2 * tok, half), BF)] * 3,
        order,
        *operands,
        flops=10 * per_block,
    )
    got_z = move(send_z, over_z)
    got_x = [move(send_x[d], over_x(d + 1)) for d in range(3)]
    kept_a, kept_b = plain(
        project_keep_body,
        "project_keep",
        [sds((4 * tok, half), F32), sds((2 * tok, half), F32)],
        order,
        *operands,
        flops=6 * per_block,
    )
    keep_a, keep_b, send_b, *send_a = plain(
        add_body,
        "add",
        [sds((tok, half), F32)] * 2 + [sds((tok, half), BF)] * 4,
        order,
        kept_a,
        kept_b,
        got_z,
        *got_x,
    )
    got_a = [move(send_a[d], over_x(d + 1)) for d in range(3)]
    got_b = move(send_b, over_z)

    packed_h, mixed = norm_pack(
        routes, keep_a, keep_b, got_a, got_b, residual, gain_row, packed_g, n_exp
    )
    rows_in = trade(packed_h)

    weight_in, weight_out = expert_in[0], expert_out[0]
    arrived, grads, act, ggu, packed_back = expert_call(rows_in, weight_in, weight_out)
    back = trade(packed_back)
    packed_y = expert_y_call(act, weight_out)
    d_expert_out = contract(act, grads, 0, 0).astype(BF)[None]
    d_expert_in = contract(arrived, ggu, 0, 0).astype(BF)[None]
    back, packed_y, d_expert_out, d_expert_in = lax.optimization_barrier(
        (back, packed_y, d_expert_out, d_expert_in)
    )
    res, d_residual = combine_grads(routes, back, mixed, gain_row, cotangent, n_exp)

    same_z = [res] + [move(res, over_x(d)) for d in range(1, 4)]
    other_z = move(res, over_z)
    cut = width * 3 // 8
    left_z = [move(v[:, :cut], over_z) for v in same_z[1:]]
    right_z = [move(other_z[:, cut:], over_x(d)) for d in range(1, 4)]
    blocks = [*same_z, other_z, *left_z, *right_z]
    packed_y, *blocks = lax.optimization_barrier((packed_y, *blocks))
    y_back = trade(packed_y)

    w_give, gain_own = plain(
        weight_give_body,
        "weight_give",
        [sds((cols, width), BF), sds((8, width), F32)],
        came,
        ctx_got,
        *blocks,
        flops=16 * tok * cols * width,
    )
    w_grad_got = move(w_give, swap)
    gain_got = move(gain_own, swap)
    out_cols = width // n_ctx
    part = (cols + 32, out_cols)
    sent = plain(
        weight_own_body,
        "weight_own",
        [sds((2,) + part, BF)] * (n_ctx // 2),
        jnp.concatenate([came, lax.axis_index("ctx").reshape(1)]),
        ctx_own,
        w_grad_got,
        gain_own,
        gain_got,
        *blocks,
        flops=16 * tok * cols * width,
        scratch=[pltpu.VMEM((n_ctx,) + part, BF)],
    )
    ctx_mine, ctx_grad_give = plain(
        context_grad_body,
        "context_grad",
        [sds((chips, tok, cols), BF)] * 2,
        came,
        o_weight,
        w_got,
        *blocks,
        flops=32 * tok * cols * width,
    )
    ctx_other = move(ctx_grad_give, swap)
    over_y = [sent[0]]
    for d in range(1, n_ctx // 2):
        around = [(u, (u + 2 * d) % n_ctx) for u in range(n_ctx)]
        over_y.append(lax.ppermute(sent[d], "ctx", around))
    layer_out = combine_out(routes, gate_weights, y_back, mixed, n_exp)
    summed = sum(f.astype(F32) for f in over_y)
    other = summed[1].astype(BF)
    last = lax.ppermute(other, "ctx", [(u, u ^ 1) for u in range(n_ctx)])
    layer_out, last = lax.optimization_barrier((layer_out, last))
    final = summed[0] + last.astype(F32)
    d_o_weight = final[:cols]
    d_gain = jnp.sum(final[cols : cols + 3 * n_ctx].reshape(3, width), axis=0)

    mine = ctx_mine.reshape(chips, 1, tok, cols)
    other = ctx_other.reshape(chips, 1, tok, cols)
    d_context = jnp.where(
        core == 0,
        jnp.concatenate([mine, other], axis=1),
        jnp.concatenate([other, mine], axis=1),
    ).reshape(context.shape)
    return (layer_out, d_context, d_residual, d_o_weight, d_gain, d_expert_in, d_expert_out)


def solution(mesh):
    rows = P(("ctx", "tp"), None)
    experts = P(("ctx", "tp"), None, None)
    in_specs = (P("ctx", "tp"), rows, P("tp", None), P(), rows, rows, experts, experts, rows)
    out_specs = (rows, P("ctx", "tp"), rows, P("tp", "ctx"), P(), experts, experts)
    return jax.shard_map(
        on_device, mesh=mesh, in_specs=in_specs, out_specs=out_specs, check_vma=False
    )
```

```python
import functools

import jax
import jax.numpy as jnp
from jax import lax
from jax.experimental import pallas as pl
from jax.experimental.pallas import tpu as pltpu
from jax.sharding import PartitionSpec as P

BF = jnp.bfloat16
F32 = jnp.float32
SLOTS = 6
GROUP = 8
PACK = 3
MIB = 1024 * 1024
LANES = 128
BIG = ("expert", "expert_y", "weight_give", "weight_own", "context_grad")


def mm(a, b, da=1, db=0):
    return lax.dot_general(a, b, (((da,), (db,)), ((), ())), preferred_element_type=F32)


def contract(left_arr, right_arr, left_dim, right_dim):
    return mm(left_arr, right_arr, left_dim, right_dim)


def iota(shape, dim):
    return lax.broadcasted_iota(jnp.int32, shape, dim)


def call(body, name, out, grid, in_specs, out_specs, scratch=(), flops=0, nbytes=0):
    return pl.pallas_call(
        body,
        out_shape=out,
        grid_spec=pltpu.PrefetchScalarGridSpec(
            num_scalar_prefetch=0,
            grid=grid,
            in_specs=in_specs,
            out_specs=out_specs,
            scratch_shapes=scratch,
        ),
        compiler_params=pltpu.CompilerParams(
            dimension_semantics=("arbitrary",) * len(grid), vmem_limit_bytes=(56 if name in BIG else 26) * MIB
        ),
        cost_estimate=pl.CostEstimate(flops=flops, bytes_accessed=nbytes, transcendentals=0),
        name=name,
    )


def whole(shape):
    n = len(shape)
    return pl.BlockSpec(shape, lambda i: (0,) * n)


def sds(shape, dtype):
    return jax.ShapeDtypeStruct(shape, dtype)


def slot_table(routes, n_exp):
    rows = routes.shape[0]
    lane = iota((rows, n_exp), 1)
    named = jnp.zeros((rows, n_exp), F32)
    for k in range(routes.shape[1]):
        named = named + (routes[:, k : k + 1] == lane).astype(F32)
    before = (iota((rows, rows), 0) > iota((rows, rows), 1)).astype(BF)
    rank = mm(before, named.astype(BF))
    return jnp.where(named > 0, rank, -1.0)


def gate_table(routes, gates, n_exp):
    rows = routes.shape[0]
    lane = iota((rows, n_exp), 1)
    table = jnp.zeros((rows, n_exp), F32)
    for k in range(routes.shape[1]):
        table = table + jnp.where(routes[:, k : k + 1] == lane, gates[:, k : k + 1], 0.0)
    return table


def thirds(values):
    high = values.astype(BF)
    rest = values - high.astype(F32)
    middle = rest.astype(BF)
    low = (rest - middle.astype(F32)).astype(BF)
    return high, middle, low


def pick_rows(slot, first, count):
    rows, n_exp = slot.shape
    row = iota((count, n_exp), 0) + first
    spread = (row // GROUP == iota((count, n_exp), 1)).astype(BF)
    at = mm(spread, slot.astype(BF), 1, 1)
    place = (iota((count, rows), 0) % GROUP).astype(F32)
    main = (at == place) & (place < SLOTS)
    tails = [(at == (place - SLOTS) * PACK + c) & (place >= SLOTS) for c in range(PACK)]
    return spread, main, tails


def pack_tokens(values, main, tails, quarter):
    out = []
    last = values[:, PACK * quarter :]
    for c in range(PACK):
        pick = jnp.concatenate([main.astype(BF), tails[c].astype(BF)], axis=1)
        source = jnp.concatenate([values[:, c * quarter : (c + 1) * quarter], last], axis=0)
        out.append(mm(pick, source))
    return out


def block_perm(count):
    real = count * SLOTS // GROUP
    row, col = iota((real, count), 0), iota((real, count), 1)
    owner, slot = row // SLOTS, row % SLOTS
    same = owner == col // GROUP
    place = col % GROUP
    main = same & (place == slot)
    tails = [
        same & (place == SLOTS + slot // PACK) & (slot % PACK == c) for c in range(PACK)
    ]
    return main.astype(BF), [t.astype(BF) for t in tails]


def block_perm_back(count):
    real = count * SLOTS // GROUP
    row, col = iota((count, real), 0), iota((count, real), 1)
    place, slot = row % GROUP, col % SLOTS
    same = row // GROUP == col // SLOTS
    main = same & (place == slot)
    tails = [
        same & (place == SLOTS + slot // PACK) & (slot % PACK == c) for c in range(PACK)
    ]
    return [jnp.concatenate([main.astype(BF), t.astype(BF)], axis=1) for t in tails]


def unpack(packed, perm, quarter):
    main, tails = perm
    head = mm(main, packed).astype(BF)
    stack = jnp.concatenate([packed[:, c * quarter : (c + 1) * quarter] for c in range(PACK)], axis=0)
    tail = mm(jnp.concatenate(tails, axis=1), stack).astype(BF)
    return jnp.concatenate([head, tail], axis=1)


def repack(rows, perm, quarter):
    last = rows[:, PACK * quarter :]
    out = []
    for c in range(PACK):
        source = jnp.concatenate([rows[:, c * quarter : (c + 1) * quarter], last], axis=0)
        out.append(mm(perm[c], source).astype(BF))
    return jnp.concatenate(out, axis=1)


def pack_grads_body(n_exp, rows, routes, gates, cot, out, slot, high, middle, low):
    i = pl.program_id(0)

    @pl.when(i == 0)
    def _():
        slot[...] = slot_table(routes[...], n_exp)
        high[...], middle[...], low[...] = thirds(gate_table(routes[...], gates[...], n_exp))

    quarter = cot.shape[1] // 4
    spread, main, tails = pick_rows(slot[...], i * rows, rows)
    gate = (mm(spread, high[...], 1, 1) + mm(spread, middle[...], 1, 1)) + mm(spread, low[...], 1, 1)
    parts = pack_tokens(cot[...], main, tails, quarter)
    for c in range(PACK):
        own = jnp.sum(jnp.where(main | tails[c], gate, 0.0), axis=1, keepdims=True)
        out[:, c * quarter : (c + 1) * quarter] = (parts[c] * own).astype(BF)


def pack_grads(routes, gates, cot, n_exp):
    tok, width = cot.shape
    total, steps = n_exp * GROUP, 4
    rows = total // steps
    table = pltpu.VMEM((tok, n_exp), BF)
    return call(
        functools.partial(pack_grads_body, n_exp, rows),
        "pack_grads",
        sds((total, width * 3 // 4), BF),
        (steps,),
        [whole(routes.shape), whole(gates.shape), whole(cot.shape)],
        pl.BlockSpec((rows, width * 3 // 4), lambda i: (i, 0)),
        [pltpu.VMEM((tok, n_exp), F32), table, table, table],
        flops=2 * total * 2 * tok * width,
        nbytes=8 * total * width,
    )(routes, gates, cot)


def norm_pack_body(n_exp, rows, routes, keep_a, keep_b, *refs):
    got_a, got_b, residual, gain, packed_g, out, mixed_out, slot, normed_h = (
        refs[:3], refs[3], *refs[4:]
    )
    i = pl.program_id(0)

    @pl.when(i == 0)
    def _():
        slot[...] = slot_table(routes[...], n_exp)
        tok, width = residual.shape
        step = 32

        def norm(j, carry):
            at = pl.ds(pl.multiple_of(j * step, step), step)
            left = keep_a[at, :]
            for part in got_a:
                left = left + part[at, :].astype(F32)
            right = keep_b[at, :] + got_b[at, :].astype(F32)
            total = jnp.concatenate([left, right], axis=1)
            mixed = (residual[at, :].astype(F32) + total).astype(BF)
            mixed_out[at, :] = mixed
            mixed = mixed.astype(F32)
            inv_rms = lax.rsqrt(jnp.mean(mixed * mixed, axis=-1, keepdims=True) + 1e-06)
            normed_h[at, :] = (mixed * inv_rms * gain[...].astype(F32)).astype(BF)
            return carry

        lax.fori_loop(0, tok // step, norm, 0)

    quarter = residual.shape[1] // 4
    _, main, tails = pick_rows(slot[...], i * rows, rows)
    packed = pack_tokens(normed_h[...], main, tails, quarter)
    for c in range(PACK):
        out[:, c * quarter : (c + 1) * quarter] = packed[c].astype(BF)
    out[:, PACK * quarter :] = packed_g[...]


def norm_pack(routes, keep_a, keep_b, got_a, got_b, residual, gain, packed_g, n_exp):
    tok, width = residual.shape
    total, steps = n_exp * GROUP, 4
    rows = total // steps
    args = (routes, keep_a, keep_b, *got_a, got_b, residual, gain)
    return call(
        functools.partial(norm_pack_body, n_exp, rows),
        "norm_pack",
        (sds((total, width * 3 // 2), BF), sds((tok, width), BF)),
        (steps,),
        [whole(a.shape) for a in args] + [pl.BlockSpec((rows, width * 3 // 4), lambda i: (i, 0))],
        (pl.BlockSpec((rows, width * 3 // 2), lambda i: (i, 0)), whole((tok, width))),
        [pltpu.VMEM((tok, n_exp), F32), pltpu.VMEM((tok, width), BF)],
        flops=2 * total * 2 * tok * width,
        nbytes=8 * total * width,
    )(*args, packed_g)


def pick_tokens(slot):
    rows, n_exp = slot.shape
    total = n_exp * GROUP
    spread = (iota((n_exp, total), 1) // GROUP == iota((n_exp, total), 0)).astype(BF)
    at = mm(slot.astype(BF), spread)
    place = (iota((rows, total), 1) % GROUP).astype(F32)
    main = (at == place) & (place < SLOTS)
    tails = [(at == (place - SLOTS) * PACK + c) & (place >= SLOTS) for c in range(PACK)]
    return spread, main, tails


def combine_grads_body(n_exp, routes, packed, mixed_ref, gain, cot, out, res_out):
    tok, width = cot.shape
    quarter = width // 4
    _, main, tails = pick_tokens(slot_table(routes[...], n_exp))
    heads, last = [], jnp.zeros((tok, quarter), F32)
    for c in range(PACK):
        pick = jnp.concatenate([main.astype(BF), tails[c].astype(BF)], axis=0)
        both = mm(pick, packed[:, c * quarter : (c + 1) * quarter])
        heads.append(both[:tok])
        last = last + both[tok:]
    grad_h = jnp.concatenate(heads + [last], axis=1)
    mixed = mixed_ref[...].astype(F32)
    inv_rms = lax.rsqrt(jnp.mean(mixed * mixed, axis=-1, keepdims=True) + 1e-06)
    normed = mixed * inv_rms
    d_gain = jnp.sum(grad_h * normed, axis=0, keepdims=True)
    gain_cols = jnp.zeros((tok, LANES), F32)
    row = iota((tok, LANES), 0)
    per = width // LANES
    for p, part in enumerate(thirds(d_gain)):
        for q in range(per):
            piece = part[:, q * LANES : (q + 1) * LANES].astype(F32)
            gain_cols = jnp.where(row == p * per + q, piece, gain_cols)
    grad_n = grad_h * gain[...].astype(F32)
    inner = jnp.mean(grad_n * normed, axis=-1, keepdims=True)
    d_res = cot[...].astype(F32) + inv_rms * (grad_n - normed * inner)
    d_res = d_res.astype(BF)
    res_out[...] = d_res
    out[:, :width] = d_res
    out[:, width:] = gain_cols.astype(BF)


def combine_grads(routes, packed, mixed, gain, cot, n_exp):
    tok, width = cot.shape
    return call(
        functools.partial(combine_grads_body, n_exp),
        "combine_grads",
        (sds((tok, width + LANES), BF), sds((tok, width), BF)),
        (1,),
        [whole(a.shape) for a in (routes, packed, mixed, gain, cot)],
        (whole((tok, width + LANES)), whole((tok, width))),
        flops=2 * packed.shape[0] * 2 * tok * width,
        nbytes=8 * packed.shape[0] * width,
    )(routes, packed, mixed, gain, cot)


def combine_out_body(n_exp, routes, gates, packed, mixed, out):
    tok, width = mixed.shape
    quarter = width // 4
    spread, main, tails = pick_tokens(slot_table(routes[...], n_exp))
    parts = thirds(gate_table(routes[...], gates[...], n_exp))
    gate = (mm(parts[0], spread) + mm(parts[1], spread)) + mm(parts[2], spread)
    high = gate.astype(BF)
    low = (gate - high.astype(F32)).astype(BF)
    none = jnp.zeros_like(high)
    last = jnp.zeros((tok, quarter), F32)
    for c in range(PACK):
        pick = jnp.concatenate(
            [
                jnp.where(main, high, none),
                jnp.where(main, low, none),
                jnp.where(tails[c], high, none),
                jnp.where(tails[c], low, none),
            ],
            axis=0,
        )
        both = mm(pick, packed[:, c * quarter : (c + 1) * quarter])
        at = slice(c * quarter, (c + 1) * quarter)
        head = both[:tok] + both[tok : 2 * tok]
        out[:, at] = (mixed[:, at].astype(F32) + head).astype(BF)
        last = last + (both[2 * tok : 3 * tok] + both[3 * tok :])
    at = slice(PACK * quarter, width)
    out[:, at] = (mixed[:, at].astype(F32) + last).astype(BF)


def combine_out(routes, gates, packed, mixed, n_exp):
    tok, width = mixed.shape
    return call(
        functools.partial(combine_out_body, n_exp),
        "combine_out",
        sds((tok, width), BF),
        (1,),
        [whole(a.shape) for a in (routes, gates, packed, mixed)],
        whole((tok, width)),
        flops=2 * packed.shape[0] * 4 * tok * width,
        nbytes=6 * packed.shape[0] * width,
    )(routes, gates, packed, mixed)


SUB = 256


def unpack_rows(packed, quarter):
    perm = block_perm(SUB)
    return jnp.concatenate(
        [
            unpack(packed[j * SUB : (j + 1) * SUB, :], perm, quarter)
            for j in range(packed.shape[0] // SUB)
        ],
        axis=0,
    )


def repack_rows(rows, out, quarter):
    perm = block_perm_back(SUB)
    real = SUB * SLOTS // GROUP
    for j in range(rows.shape[0] // real):
        out[j * SUB : (j + 1) * SUB, :] = repack(rows[j * real : (j + 1) * real, :], perm, quarter)


def expert_body(
    packed_h, packed_g, weight_in, weight_out, rows_out, grads_out, act_out, ggu_out, packed_out
):
    width, both = weight_in.shape
    hidden = both // 2
    quarter = width // 4
    rows = unpack_rows(packed_h, quarter)
    rows_out[...] = rows
    gate_part = mm(rows, weight_in[:, :hidden])
    up_part = mm(rows, weight_in[:, hidden:])
    sigma = jax.nn.sigmoid(gate_part)
    silu = gate_part * sigma
    act_out[...] = (silu * up_part).astype(BF)
    grads = unpack_rows(packed_g, quarter)
    grads_out[...] = grads
    grad_act = mm(grads, weight_out[...], 1, 1)
    grad_gate = (grad_act * up_part * sigma * (1.0 + gate_part * (1.0 - sigma))).astype(BF)
    grad_up = (grad_act * silu).astype(BF)
    ggu_out[:, :hidden] = grad_gate
    ggu_out[:, hidden:] = grad_up
    back = mm(jnp.concatenate([grad_gate, grad_up], axis=1), weight_in[...], 1, 1).astype(BF)
    repack_rows(back, packed_out, quarter)


def once(shape):
    n = len(shape)
    return pl.BlockSpec(shape, lambda i: (0,) * n, pipeline_mode=pl.Buffered(buffer_count=1))


def expert_call(packed, weight_in, weight_out):
    width, both = weight_in.shape
    hidden = both // 2
    steps = 2
    block = packed.shape[0] // steps
    real = block * SLOTS // GROUP
    part = packed.shape[1] // 2
    at = lambda i: (i, 0)
    return call(
        expert_body,
        "expert",
        (
            sds((real * steps, width), BF),
            sds((real * steps, width), BF),
            sds((real * steps, hidden), BF),
            sds((real * steps, both), BF),
            sds((packed.shape[0], part), BF),
        ),
        (steps,),
        [
            pl.BlockSpec((block, part), at),
            pl.BlockSpec((block, part), lambda i: (i, 1)),
            once(weight_in.shape),
            once(weight_out.shape),
        ],
        (
            pl.BlockSpec((real, width), at),
            pl.BlockSpec((real, width), at),
            pl.BlockSpec((real, hidden), at),
            pl.BlockSpec((real, both), at),
            pl.BlockSpec((block, part), at),
        ),
        flops=5 * real * steps * both * width,
        nbytes=2 * both * width + 10 * real * steps * width,
    )(packed, packed, weight_in, weight_out)


def expert_y_body(act, weight_out, packed_out):
    rows = mm(act[...], weight_out[...]).astype(BF)
    repack_rows(rows, packed_out, weight_out.shape[1] // 4)


def expert_y_call(act, weight_out):
    hidden, width = weight_out.shape
    steps = 2
    real = act.shape[0] // steps
    block = real * GROUP // SLOTS
    at = lambda i: (i, 0)
    return call(
        expert_y_body,
        "expert_y",
        sds((block * steps, width * 3 // 4), BF),
        (steps,),
        [pl.BlockSpec((real, hidden), at), whole(weight_out.shape)],
        pl.BlockSpec((block, width * 3 // 4), at),
        flops=2 * real * steps * hidden * width,
        nbytes=2 * hidden * width + 4 * real * steps * width,
    )(act, weight_out)


def rows_of(ref, order, places):
    return jnp.concatenate([ref[order[p]] for p in places], axis=0)


def product(order, places, ctx_own, ctx_got, w_own, w_got, cols):
    own = mm(rows_of(ctx_own, order, places), w_own[:, cols])
    return own + mm(rows_of(ctx_got, order, places), w_got[:, cols])


def halves(w):
    half = w.shape[1] // 2
    return slice(0, half), slice(half, 2 * half)


def project_first_body(order, ctx_own, ctx_got, w_own, w_got, over_z, *over_x):
    left, right = halves(w_own)
    args = (ctx_own, ctx_got, w_own, w_got)
    over_z[...] = product(order, [1, 3, 5, 7], *args, left).astype(BF)
    for d in range(3):
        over_x[d][...] = product(order, [2 * d + 2, 2 * d + 3], *args, right).astype(BF)


def project_keep_body(order, ctx_own, ctx_got, w_own, w_got, keep_a, keep_b):
    left, right = halves(w_own)
    args = (ctx_own, ctx_got, w_own, w_got)
    keep_b[...] = product(order, [0, 1], *args, right)
    keep_a[...] = product(order, [0, 2, 4, 6], *args, left)


def add_body(order, kept_a, kept_b, got_z, got_1, got_2, got_3, keep_a, keep_b, over_z, *over_x):
    tok = keep_a.shape[0]
    keep_a[...] = kept_a[0:tok, :] + got_z[0:tok, :].astype(F32)
    for d in range(3):
        at = slice((d + 1) * tok, (d + 2) * tok)
        over_x[d][...] = (kept_a[at, :] + got_z[at, :].astype(F32)).astype(BF)
    total = kept_b[...]
    for got in (got_1, got_2, got_3):
        total = total + got[...].astype(F32)
    keep_b[...] = total[:tok]
    over_z[...] = total[tok:].astype(BF)


def plain(body, name, outs, order, *args, flops=0, scratch=()):
    nbytes = sum(a.size * a.dtype.itemsize for a in args)
    nbytes += sum(o.size * o.dtype.itemsize for o in outs)
    return call(
        body,
        name,
        tuple(outs),
        (1,),
        [pl.BlockSpec(memory_space=pltpu.SMEM)] + [whole(a.shape) for a in args],
        tuple(whole(o.shape) for o in outs),
        scratch,
        flops=flops,
        nbytes=nbytes,
    )(order, *args)


N_BLOCKS = 11


def gather_rows(blocks):
    same_z, other_z, left_z, right_z = blocks[:4], blocks[4], blocks[5:8], blocks[8:]
    width, cut = other_z.shape[1] - LANES, left_z[0].shape[1]
    left, right = [], []
    for d in range(4):
        left += [same_z[d][:, :cut], left_z[d - 1][...] if d else other_z[:, :cut]]
        right += [same_z[d][:, cut:width]]
        right += [right_z[d - 1][:, : width - cut] if d else other_z[:, cut:width]]
    return jnp.concatenate(left, axis=0), jnp.concatenate(right, axis=0)


def gather_gain(blocks):
    total = jnp.zeros((blocks[0].shape[0], LANES), F32)
    for block in blocks[:5] + blocks[8:]:
        total = total + block[:, block.shape[1] - LANES :].astype(F32)
    per = (blocks[0].shape[1] - LANES) // LANES
    rows = []
    for q in range(per):
        high, middle, low = [total[p * per + q : p * per + q + 1, :] for p in range(3)]
        rows.append(high + middle + low)
    return jnp.concatenate(rows, axis=1)


def weight_give_body(order, ctx_got, *refs):
    blocks, (give, gain_out) = refs[:N_BLOCKS], refs[N_BLOCKS:]
    ctx = rows_of(ctx_got, order, range(8))
    first = 0
    for rows in gather_rows(blocks):
        last = first + rows.shape[1]
        give[:, first:last] = mm(ctx, rows, 0, 0).astype(BF)
        first = last
    gain_out[...] = jnp.broadcast_to(gather_gain(blocks), gain_out.shape)


def context_grad_body(order, w_own, w_got, *refs):
    blocks, (own, give) = refs[:N_BLOCKS], refs[N_BLOCKS:]
    tok = own.shape[1]
    left, right = gather_rows(blocks)
    cut = left.shape[1]
    for w, out in ((w_got, give), (w_own, own)):
        grad = mm(left, w[:, :cut], 1, 1) + mm(right, w[:, cut:], 1, 1)
        grad = grad.astype(BF)
        for p in range(8):
            out[order[p] // 2] = grad[p * tok : (p + 1) * tok]


def weight_own_body(order, ctx_own, got, gain_own, gain_got, *refs):
    blocks, outs, held = refs[:N_BLOCKS], refs[N_BLOCKS:-1], refs[-1]
    cols = ctx_own.shape[2]
    n_ctx, _, width = held.shape
    ctx = rows_of(ctx_own, order, range(8))
    parts = thirds(gain_own[0:1, :] + gain_got[0:1, :])
    row = iota((16, width), 0)
    gain = jnp.zeros((16, width), F32)
    for p in range(2):
        for j in range(n_ctx):
            piece = parts[p][:, j * width : (j + 1) * width].astype(F32)
            gain = jnp.where(row == p * n_ctx + j, piece, gain)
    gain = gain.astype(BF)
    first = 0
    for rows in gather_rows(blocks):
        last = first + rows.shape[1]
        grad = mm(ctx, rows, 0, 0) + got[:, first:last].astype(F32)
        grad = grad.astype(BF)
        for j in range(first // width, last // width):
            held[j, 0:cols, :] = grad[:, j * width - first : (j + 1) * width - first]
            held[j, cols : cols + 16, :] = gain
        first = last
    y, z = order[8] // 2, order[8] % 2
    for d, out in enumerate(outs):
        for o in range(2):
            out[o] = held[(y + d) % (n_ctx // 2) * 2 + (z + o) % 2]


def trade(values):
    n_all = lax.axis_size("ctx") * lax.axis_size("tp")
    shaped = values.reshape(n_all, GROUP, values.shape[1])
    moved = lax.all_to_all(shaped, ("ctx", "tp"), split_axis=0, concat_axis=0, tiled=True)
    return moved.reshape(values.shape)


def on_device(
    context, residual, o_weight, norm_gain, routes, gate_weights, expert_in, expert_out, cotangent
):
    tok, width = residual.shape
    n_tp = lax.axis_size("tp")
    n_ctx = lax.axis_size("ctx")
    n_exp = n_tp * n_ctx
    chips = n_tp // 2
    cols = context.shape[1]
    core = lax.axis_index("tp") % 2
    gain_row = norm_gain.reshape(1, width)

    t = lax.axis_index("tp")
    x, z = t // 4, t // 2 % 2
    pairs = [(d, o) for d in range(4) for o in range(2)]
    order = jnp.stack([(x + d) % 4 * 4 + (z ^ o) * 2 + core for d, o in pairs])
    came = jnp.stack([(x - d) % 4 * 4 + (z ^ o) * 2 + core for d, o in pairs])

    def over_x(d):
        return [(u, (u + 4 * d) % n_tp) for u in range(n_tp)]

    over_z = [(u, u ^ 2) for u in range(n_tp)]
    swap = [(u, u ^ 1) for u in range(n_tp)]

    def move(values, perm):
        return lax.ppermute(values, "tp", perm)

    ctx_own = context.reshape(n_tp, tok, cols)
    ctx_got = move(ctx_own, swap)
    w_got = move(o_weight, swap)
    packed_g = pack_grads(routes, gate_weights, cotangent, n_exp)
    half = width // 2
    operands = (ctx_own, ctx_got, o_weight, w_got)
    per_block = 4 * tok * cols * half
    send_z, *send_x = plain(
        project_first_body,
        "project_first",
        [sds((4 * tok, half), BF)] + [sds((2 * tok, half), BF)] * 3,
        order,
        *operands,
        flops=10 * per_block,
    )
    got_z = move(send_z, over_z)
    got_x = [move(send_x[d], over_x(d + 1)) for d in range(3)]
    kept_a, kept_b = plain(
        project_keep_body,
        "project_keep",
        [sds((4 * tok, half), F32), sds((2 * tok, half), F32)],
        order,
        *operands,
        flops=6 * per_block,
    )
    keep_a, keep_b, send_b, *send_a = plain(
        add_body,
        "add",
        [sds((tok, half), F32)] * 2 + [sds((tok, half), BF)] * 4,
        order,
        kept_a,
        kept_b,
        got_z,
        *got_x,
    )
    got_a = [move(send_a[d], over_x(d + 1)) for d in range(3)]
    got_b = move(send_b, over_z)

    packed_h, mixed = norm_pack(
        routes, keep_a, keep_b, got_a, got_b, residual, gain_row, packed_g, n_exp
    )
    rows_in = trade(packed_h)

    weight_in, weight_out = expert_in[0], expert_out[0]
    arrived, grads, act, ggu, packed_back = expert_call(rows_in, weight_in, weight_out)
    back = trade(packed_back)
    packed_y = expert_y_call(act, weight_out)
    d_expert_out = contract(act, grads, 0, 0).astype(BF)[None]
    d_expert_in = contract(arrived, ggu, 0, 0).astype(BF)[None]
    back, packed_y, d_expert_out, d_expert_in = lax.optimization_barrier(
        (back, packed_y, d_expert_out, d_expert_in)
    )
    res, d_residual = combine_grads(routes, back, mixed, gain_row, cotangent, n_exp)

    same_z = [res] + [move(res, over_x(d)) for d in range(1, 4)]
    other_z = move(res, over_z)
    cut = width * 3 // 8
    left_z = [move(v[:, :cut], over_z) for v in same_z[1:]]
    right_z = [move(other_z[:, cut:], over_x(d)) for d in range(1, 4)]
    blocks = [*same_z, other_z, *left_z, *right_z]
    packed_y, *blocks = lax.optimization_barrier((packed_y, *blocks))
    y_back = trade(packed_y)

    w_give, gain_own = plain(
        weight_give_body,
        "weight_give",
        [sds((cols, width), BF), sds((8, width), F32)],
        came,
        ctx_got,
        *blocks,
        flops=16 * tok * cols * width,
    )
    w_grad_got = move(w_give, swap)
    gain_got = move(gain_own, swap)
    out_cols = width // n_ctx
    part = (cols + 16, out_cols)
    sent = plain(
        weight_own_body,
        "weight_own",
        [sds((2,) + part, BF)] * (n_ctx // 2),
        jnp.concatenate([came, lax.axis_index("ctx").reshape(1)]),
        ctx_own,
        w_grad_got,
        gain_own,
        gain_got,
        *blocks,
        flops=16 * tok * cols * width,
        scratch=[pltpu.VMEM((n_ctx,) + part, BF)],
    )
    ctx_mine, ctx_grad_give = plain(
        context_grad_body,
        "context_grad",
        [sds((chips, tok, cols), BF)] * 2,
        came,
        o_weight,
        w_got,
        *blocks,
        flops=32 * tok * cols * width,
    )
    ctx_other = move(ctx_grad_give, swap)
    over_y = [sent[0]]
    for d in range(1, n_ctx // 2):
        around = [(u, (u + 2 * d) % n_ctx) for u in range(n_ctx)]
        over_y.append(lax.ppermute(sent[d], "ctx", around))
    layer_out = combine_out(routes, gate_weights, y_back, mixed, n_exp)
    layer_out, *over_y = lax.optimization_barrier((layer_out, *over_y))
    summed = sum(f.astype(F32) for f in over_y)
    other = summed[1].astype(BF)
    last = lax.ppermute(other, "ctx", [(u, u ^ 1) for u in range(n_ctx)])
    final = summed[0] + last.astype(F32)
    d_o_weight = final[:cols]
    d_gain = jnp.sum(final[cols : cols + 2 * n_ctx].reshape(2, width), axis=0)

    mine = ctx_mine.reshape(chips, 1, tok, cols)
    other = ctx_other.reshape(chips, 1, tok, cols)
    d_context = jnp.where(
        core == 0,
        jnp.concatenate([mine, other], axis=1),
        jnp.concatenate([other, mine], axis=1),
    ).reshape(context.shape)
    return (layer_out, d_context, d_residual, d_o_weight, d_gain, d_expert_in, d_expert_out)


def solution(mesh):
    rows = P(("ctx", "tp"), None)
    experts = P(("ctx", "tp"), None, None)
    in_specs = (P("ctx", "tp"), rows, P("tp", None), P(), rows, rows, experts, experts, rows)
    out_specs = (rows, P("ctx", "tp"), rows, P("tp", "ctx"), P(), experts, experts)
    return jax.shard_map(
        on_device, mesh=mesh, in_specs=in_specs, out_specs=out_specs, check_vma=False
    )
```
